512 devices in a mesh: tile: 64 (over z, y), group: 8 (over x, core).
Axes of the slice: x: 4, y: 8, z: 8, core: 2. Of those that a mesh axis runs over, the one named last changes fastest.
Arguments:
- object_field: float32 [2, 2048, 16384], P(None, None, 'tile'), may hold values from -6 to 6
- probe: float32 [2, 256, 256], replicated, may hold values from -6 to 6
- amplitudes: bfloat16 [3072, 256, 256], P(('tile', 'group')), may hold values from 0.5 to 3
- row_offset: int32 [3072], P(('tile', 'group')), may hold values from 0 to 1792
- col_offset: int32 [3072], P(('tile', 'group')), may hold values from 0 to 255
- counts: int32 [512], P(('tile', 'group')), may hold values from 1 to 6, as said below
Outputs:
- updated_object: float32 [2, 2048, 16384], P(None, None, 'tile')
The draws below stay inside these ranges and needn't reach their ends.
Inputs may be any that keep to these rules, and one draw needn't show every extreme that they name: counts[s] live patterns are the first slots of slot set s; the slots after them are ignored.
All inputs are finite; a program needn't handle non-finite values.
Results may differ from the reference program's by a relative error of at most 0.0003.
Values sent between devices are 32-bit elements; how exact they have to be, the bound alone decides.
No kernel may reach another device: no remote copies, remote signals or barrier semaphores. Data moves between devices by JAX's collectives and lax.ppermute only.
A program may use at most 128 MiB of HBM per device.

```python
import jax
import jax.numpy as jnp
from jax import lax

M = 256
TH = 2048
TW = 256
PAT_DEV = 6
W = 16384
SLOTS = 512
PER_TILE = 48
NPAT = 3072


def draw_counts(key, part):
    key = jax.random.fold_in(key, 11)
    first, second, third = jax.random.split(key, 3)
    busy = jax.random.randint(first, (SLOTS,), 0, 6) == 0
    lower = jax.random.randint(second, (SLOTS,), 1, max(PAT_DEV // 3, 1) + 1)
    values = jnp.where(busy, PAT_DEV, lower)
    chosen = jax.random.randint(third, (), 0, SLOTS)
    values = jnp.where(jnp.arange(SLOTS) == chosen, PAT_DEV, values)
    return values.astype(jnp.int32)


def plant(array, own_key, least, largest):
    longest = array.shape.index(max(array.shape))
    spots = []
    for shift in (0, 1):
        where = [jax.random.randint(jax.random.fold_in(own_key, axis), (), 0, length) for axis, length in enumerate(array.shape)]
        where[longest] = (where[longest] + shift) % array.shape[longest]
        spots.append(tuple(where))
    return array.at[spots[0]].set(least).at[spots[1]].set(largest)


def block_scale(own_key, dims, pieces, least, high):
    level = 1.0
    for dim, shards_of in pieces:
        heights = jax.random.uniform(jax.random.fold_in(jax.random.fold_in(own_key, 6), dim), (shards_of,), jnp.float32, least / len(pieces), high / len(pieces))
        level = level * jnp.repeat(jnp.exp(heights), dims[dim] // shards_of).reshape((-1,) + (1,) * (len(dims) - 1 - dim))
    return level


def gaussian(rng, dims, spread, bound, cuts=(), dtype=jnp.bfloat16):
    array = spread * jax.random.normal(rng, dims, jnp.float32)
    if cuts:
        array = array * block_scale(rng, dims, cuts, -0.22, 0.18)
    return jnp.clip(array, -bound, bound).astype(dtype)


def setup_inputs(seed: int = 0) -> dict:
    arg_keys = jax.random.split(jax.random.key(seed), 7)
    return {
        "object_field": gaussian(arg_keys[0], (2, TH, W), 1.0, 6.0, ((2, 64),), jnp.float32),
        "probe": gaussian(arg_keys[1], (2, M, M), 1.0, 6.0, (), jnp.float32),
        "amplitudes": jnp.clip(0.5 + 2.5 * jax.random.uniform(arg_keys[2], (NPAT, M, M), jnp.float32) ** block_scale(arg_keys[2], (NPAT, M, M), ((0, 512),), -0.2, 0.2), 0.5, 3.0).astype(jnp.bfloat16),
        "row_offset": plant(jax.random.randint(arg_keys[3], (NPAT,), 0, TH - M + 1), jax.random.fold_in(arg_keys[3], 1), 0, TH - M).astype(jnp.int32),
        "col_offset": plant(jax.random.randint(arg_keys[4], (NPAT,), 0, TW), jax.random.fold_in(arg_keys[4], 1), 0, TW - 1).astype(jnp.int32),
        "counts": draw_counts(jax.random.fold_in(arg_keys[6], 71), 0),
    }


FLOOR = 0.25
REG = 0.5


def reference(object_field, probe, amplitudes, row_offset, col_offset, counts):
    padded = jnp.concatenate([object_field, jnp.zeros((2, TH, M), jnp.float32)], axis=2)
    probe_c = lax.complex(probe[0], probe[1])
    intensity = probe[0] * probe[0] + probe[1] * probe[1]
    zero = jnp.zeros((), jnp.int32)
    maps_start = jnp.zeros((3, TH, W + M), jnp.float32)

    def step(index, maps):
        index = jnp.asarray(index).astype(jnp.int32)
        tile_no = index // PER_TILE
        live = (index % PAT_DEV < counts[index // PAT_DEV]).astype(jnp.float32)
        row = row_offset[index].astype(jnp.int32)
        col = (tile_no * TW + col_offset[index]).astype(jnp.int32)
        window = lax.dynamic_slice(padded, (zero, row, col), (2, M, M))
        exit_wave = probe_c * lax.complex(window[0], window[1])
        far = jnp.fft.fft2(exit_wave, norm="ortho")
        factor = amplitudes[index].astype(jnp.float32) / jnp.maximum(jnp.abs(far), FLOOR) - 1.0
        back = jnp.fft.ifft2(far * factor, norm="ortho")
        grad = jnp.conj(probe_c) * back
        contrib = jnp.stack([jnp.real(grad), jnp.imag(grad), intensity]) * live
        current = lax.dynamic_slice(maps, (zero, row, col), (3, M, M))
        return lax.dynamic_update_slice(maps, current + contrib, (zero, row, col))

    maps = lax.fori_loop(0, NPAT, step, maps_start)
    maps = maps[:, :, :W]
    return object_field + maps[0:2] / (maps[2:3] + REG)
```

```python
import functools
import math

import jax
import jax.numpy as jnp
import numpy as np
from jax import lax
from jax.experimental import pallas as pl
from jax.experimental.pallas import tpu as pltpu
from jax.sharding import PartitionSpec as P

FLOOR = 0.25
REG = 0.5
SUB = 8
MIB = 2**20

STEPS = (0, -2, 2, 4)


def tables(length):
    steps = np.arange(length)
    angle = (steps[:, None] * steps[None, :] % length) * (2.0 * math.pi / length)
    factor = 1.0 / math.sqrt(length)
    cos, sin = np.cos(angle) * factor, np.sin(angle) * factor
    parts = []
    for table in (cos, cos - sin, cos + sin):
        table = table.astype(np.float32)
        high = table.astype(jnp.bfloat16)
        low = (table - high.astype(np.float32)).astype(jnp.bfloat16)
        parts += [high, low]
    return np.stack(parts)


def split(x):
    high = x.astype(jnp.bfloat16)
    return high, (x - high.astype(jnp.float32)).astype(jnp.bfloat16)


def dot(a, b):
    return jnp.dot(a, b, preferred_element_type=jnp.float32)


def right(x, tab, which):
    high, low = split(x)
    th, tl = tab[2 * which], tab[2 * which + 1]
    return dot(high, th) + dot(low, th) + dot(high, tl)


def left(x, tab, which):
    high, low = split(x)
    th, tl = tab[2 * which], tab[2 * which + 1]
    return dot(th, high) + dot(th, low) + dot(tl, high)


def forward(mul, a, b, tab):
    both = mul(a + b, tab, 0)
    return both - mul(b, tab, 1), both - mul(a, tab, 2)


def inverse(mul, a, b, tab):
    both = mul(a + b, tab, 0)
    return both - mul(b, tab, 2), both - mul(a, tab, 1)


def class_of(group, step, other, parts):
    index = (group + step) & (parts - 1)
    return index ^ 1 if other else index


def patterns_kernel(size, rows, parts, slots, group_ref, row_ref, col_ref, count_ref, own_ref, probe_hbm, amp_hbm, tab_hbm, *refs):
    pieces, refs = refs[:parts], refs[parts:]
    out_ref, own_buf, rim_buf, probe_ref, amp_ref, tab_ref, stage, own_sems, fixed_sems, piece_sems, store_sems = refs
    group, count = group_ref[0], count_ref[0]
    span = size + SUB
    depth = size // parts

    def start_of(p):
        return pl.multiple_of(row_ref[p] & -SUB, SUB)

    def first_of(p):
        return pl.multiple_of(jnp.minimum(start_of(p), rows - span), SUB)

    def load(p):
        slot = lax.rem(p, 2)
        return pltpu.make_async_copy(own_ref.at[:, pl.ds(first_of(p), span)], own_buf.at[slot], own_sems.at[slot])

    def store(p):
        where = pl.ds(pl.multiple_of(p * 2 * depth, 2 * depth), 2 * depth)
        return pltpu.make_async_copy(stage.at[:, where], out_ref.at[:, where], store_sems.at[p])

    fixed = [
        pltpu.make_async_copy(a, b, fixed_sems.at[n])
        for n, (a, b) in enumerate(((probe_hbm, probe_ref), (tab_hbm, tab_ref), (amp_hbm, amp_ref)))
    ]
    rims = []
    for n, piece in enumerate(pieces):
        index = class_of(group, STEPS[n // 2], n % 2, parts)
        rims.append(pltpu.make_async_copy(piece, rim_buf.at[:, :, index], piece_sems.at[n]))
    load(0).start()
    for copy in rims + fixed:
        copy.start()

    lane = lax.broadcasted_iota(jnp.int32, (SUB, size), 1)
    head_row = lax.broadcasted_iota(jnp.int32, (SUB, size), 0)
    column = lax.broadcasted_iota(jnp.int32, (size, size), 1)
    note = jnp.where(lane == 2 * slots, count, 0)
    for p in range(slots):
        note = jnp.where(lane == p, row_ref[p], note)
        note = jnp.where(lane == slots + p, col_ref[p], note)
    note = note.astype(jnp.float32)
    for part in range(parts):
        stage[part, slots * 2 * depth :] = note
    notes = pl.ds(slots * 2 * depth, SUB)
    last = pltpu.make_async_copy(stage.at[:, notes], out_ref.at[:, notes], store_sems.at[slots])
    last.start()
    for copy in fixed + rims:
        copy.wait()
    rim = rim_buf.reshape(2, rows, size)

    def pattern(p, _):
        slot = lax.rem(p, 2)
        row, col = row_ref[p], col_ref[p]
        base = start_of(p)
        shift = row - base

        @pl.when(p + 1 < count)
        def _():
            load(p + 1).start()

        pr, pi = [pltpu.roll(pltpu.roll(probe_ref[ch], shift, 0), col, 1) for ch in range(2)]
        mine = column >= col
        load(p).wait()
        lead = pl.multiple_of(base - first_of(p), SUB)
        tail = pl.multiple_of(jnp.minimum(lead + size, size), SUB)
        tail_rim = pl.multiple_of(jnp.minimum(base + size, rows - SUB), SUB)

        def window(ch):
            full = jnp.where(mine, own_buf[slot, ch, pl.ds(lead, size)], rim[ch, pl.ds(base, size)])
            wrap = jnp.where(mine[:SUB], own_buf[slot, ch, pl.ds(tail, SUB)], rim[ch, pl.ds(tail_rim, SUB)])
            head = jnp.where(head_row >= shift, full[:SUB], wrap)
            return jnp.concatenate([head, full[SUB:]], axis=0)

        o_re, o_im = window(0), window(1)
        a = pr * o_re - pi * o_im
        b = pr * o_im + pi * o_re
        a, b = forward(right, a, b, tab_ref)
        a, b = forward(left, a, b, tab_ref)
        factor = amp_ref[p].astype(jnp.float32) * lax.rsqrt(jnp.maximum(a * a + b * b, FLOOR * FLOOR)) - 1.0
        a, b = a * factor, b * factor
        a, b = inverse(left, a, b, tab_ref)
        a, b = inverse(right, a, b, tab_ref)
        for ch, g in enumerate((pr * a + pi * b, pr * b - pi * a)):
            for t in range(parts):
                index = ((base >> 3) + t) & (parts - 1)
                for m in range(depth // SUB):
                    at = pl.multiple_of((2 * p + ch) * depth + SUB * m, SUB)
                    block = SUB * (parts * m + t)
                    stage[index, pl.ds(at, SUB)] = g[block : block + SUB]
        store(p).start()
        return 0

    lax.fori_loop(0, count, pattern, 0)

    def stored(p, _):
        store(p).wait()
        return 0

    last.wait()
    lax.fori_loop(0, count, stored, 0)


def patterns(group, own, pieces, probe, amplitudes, row, col, count):
    rows, size = own.shape[1:]
    slots, parts = amplitudes.shape[0], len(pieces)
    depth = size // parts
    length = slots * 2 * depth + SUB
    smem = pl.BlockSpec(memory_space=pltpu.SMEM)
    hbm = pl.BlockSpec(memory_space=pl.ANY)
    tab = jnp.asarray(tables(size))
    return pl.pallas_call(
        functools.partial(patterns_kernel, size, rows, parts, slots),
        out_shape=jax.ShapeDtypeStruct((parts, length, size), jnp.float32),
        in_specs=[smem] * 4 + [hbm] * (4 + parts),
        out_specs=hbm,
        scratch_shapes=[
            pltpu.VMEM((2, 2, size + SUB, size), jnp.float32),
            pltpu.VMEM((2, rows // (SUB * parts), parts, SUB, size), jnp.float32),
            pltpu.VMEM(probe.shape, jnp.float32),
            pltpu.VMEM(amplitudes.shape, amplitudes.dtype),
            pltpu.VMEM(tab.shape, tab.dtype),
            pltpu.VMEM((parts, length, size), jnp.float32),
            pltpu.SemaphoreType.DMA((2,)),
            pltpu.SemaphoreType.DMA((3,)),
            pltpu.SemaphoreType.DMA((parts,)),
            pltpu.SemaphoreType.DMA((slots + 1,)),
        ],
        compiler_params=pltpu.CompilerParams(vmem_limit_bytes=40 * MIB),
        cost_estimate=pl.CostEstimate(flops=36 * 2 * size**3 * slots, bytes_accessed=12 * MIB, transcendentals=0),
        name="patterns",
    )(group, row, col, count, own, probe, amplitudes, tab, *pieces)


def place(row, group, parts):
    block = row >> 3
    first = (group - block) & (parts - 1)
    local = (block + first - group) >> (parts.bit_length() - 1)
    return first, pl.multiple_of(local * SUB, SUB), jnp.where(first == 0, row & (SUB - 1), 0)


def each_live(notes_ref, slots, step):
    def device(d, _):
        def pattern(p, _):
            step(d, p, notes_ref[d, p], notes_ref[d, slots + p])
            return 0

        return lax.fori_loop(0, notes_ref[d, 2 * slots], pattern, 0)

    lax.fori_loop(0, notes_ref.shape[0], device, 0)


def gather_kernel(size, parts, slots, group_ref, notes_ref, got_ref, here_ref, next_ref, total):
    depth = size // parts
    group = group_ref[0]
    total[...] = jnp.zeros_like(total)
    column = lax.broadcasted_iota(jnp.int32, (depth, size), 1)
    head_row = lax.broadcasted_iota(jnp.int32, (SUB, size), 0)

    def step(d, p, row, col):
        _, at, shift = place(row, group, parts)
        mine = column >= col
        for ch in range(2):
            block = got_ref[d, pl.ds(pl.multiple_of((2 * p + ch) * depth, depth), depth)]
            for side in range(2):
                part = jnp.where(mine if side == 0 else jnp.logical_not(mine), block, 0.0)
                head = part[:SUB]
                total[side, ch, pl.ds(at, SUB)] += jnp.where(head_row >= shift, head, 0.0)
                total[side, ch, pl.ds(at + SUB, depth - SUB)] += part[SUB:]
                total[side, ch, pl.ds(at + depth, SUB)] += jnp.where(head_row < shift, head, 0.0)

    each_live(notes_ref, slots, step)
    kept = here_ref.shape[1]
    here_ref[...] = total[0, :, :kept]
    next_ref[...] = total[1, :, :kept]


def gathered(group, notes, got, slots, kept):
    parts, length, size = got.shape
    smem = pl.BlockSpec(memory_space=pltpu.SMEM)
    vmem = pl.BlockSpec(memory_space=pltpu.VMEM)
    shape = jax.ShapeDtypeStruct((2, kept, size), jnp.float32)
    return pl.pallas_call(
        functools.partial(gather_kernel, size, parts, slots),
        out_shape=(shape, shape),
        in_specs=[smem, smem, vmem],
        out_specs=(vmem, vmem),
        scratch_shapes=[pltpu.VMEM((2, 2, kept + SUB, size), jnp.float32)],
        compiler_params=pltpu.CompilerParams(vmem_limit_bytes=24 * MIB),
        cost_estimate=pl.CostEstimate(flops=2**22, bytes_accessed=6 * MIB, transcendentals=0),
        name="gathered",
    )(group, notes, got)


def illumination_kernel(size, parts, slots, group_ref, here_ref, before_ref, probe_ref, out_ref, intensity, total):
    depth = size // parts
    group = group_ref[0]
    square = probe_ref[0] * probe_ref[0] + probe_ref[1] * probe_ref[1]
    intensity[:SUB] = square[size - SUB :]
    intensity[SUB:] = square
    total[...] = jnp.zeros_like(total)
    column = lax.broadcasted_iota(jnp.int32, (depth, size), 1)
    head_row = lax.broadcasted_iota(jnp.int32, (SUB, size), 0)

    for side, ref in enumerate((here_ref, before_ref)):

        def step(d, p, row, col):
            first, at, shift = place(row, group, parts)
            down = row & (SUB - 1)
            blocks = []
            for m in range(depth // SUB):
                start = pl.multiple_of((parts * m + first) * SUB, SUB)
                above, below = [pltpu.roll(intensity[pl.ds(start + n * SUB, SUB)], down, 0) for n in range(2)]
                blocks.append(jnp.where(head_row >= down, below, above))
            placed = pltpu.roll(jnp.concatenate(blocks, axis=0), col, 1)
            part = jnp.where(column >= col if side == 0 else column < col, placed, 0.0)
            head = part[:SUB]
            total[pl.ds(at, SUB)] += jnp.where(head_row >= shift, head, 0.0)
            total[pl.ds(at + SUB, depth - SUB)] += part[SUB:]
            total[pl.ds(at + depth, SUB)] += jnp.where(head_row < shift, head, 0.0)

        each_live(ref, slots, step)
    out_ref[...] = total[: out_ref.shape[0]] + REG


def illumination(group, here, before, probe, slots, kept):
    size = probe.shape[1]
    parts = here.shape[0]
    smem = pl.BlockSpec(memory_space=pltpu.SMEM)
    vmem = pl.BlockSpec(memory_space=pltpu.VMEM)
    return pl.pallas_call(
        functools.partial(illumination_kernel, size, parts, slots),
        out_shape=jax.ShapeDtypeStruct((kept, size), jnp.float32),
        in_specs=[smem, smem, smem, vmem],
        out_specs=vmem,
        scratch_shapes=[
            pltpu.VMEM((size + SUB, size), jnp.float32),
            pltpu.VMEM((kept + SUB, size), jnp.float32),
        ],
        compiler_params=pltpu.CompilerParams(vmem_limit_bytes=16 * MIB),
        cost_estimate=pl.CostEstimate(flops=2**22, bytes_accessed=8 * MIB, transcendentals=0),
        name="illumination",
    )(group, here, before, probe)


def assemble_kernel(parts, group_ref, *refs):
    pieces, out_ref, sems = refs[:-2], refs[-2], refs[-1]
    group = group_ref[0]
    copies = []
    for n, piece in enumerate(pieces):
        whole = n < 6
        index = class_of(group, STEPS[n // 2] if whole else STEPS[3], n % 2, parts)
        place = out_ref.at[:, :, index] if whole else out_ref.at[(n - 6) // 2, :, index]
        copies.append(pltpu.make_async_copy(piece, place, sems.at[n]))
    for copy in copies:
        copy.start()
    for copy in copies:
        copy.wait()


def assembled(group, pieces, shape):
    parts = shape[2]
    return pl.pallas_call(
        functools.partial(assemble_kernel, parts),
        out_shape=jax.ShapeDtypeStruct(shape, jnp.float32),
        in_specs=[pl.BlockSpec(memory_space=pltpu.SMEM)] + [pl.BlockSpec(memory_space=pl.ANY)] * len(pieces),
        out_specs=pl.BlockSpec(memory_space=pl.ANY),
        scratch_shapes=[pltpu.SemaphoreType.DMA((len(pieces),))],
        cost_estimate=pl.CostEstimate(flops=0, bytes_accessed=8 * MIB, transcendentals=0),
        name="assembled",
    )(group, *pieces)


def passed_along(x, axis, by):
    devices = lax.axis_size(axis)
    pairs = [(i, i + by) for i in range(devices) if 0 <= i + by < devices]
    return lax.ppermute(x, axis, pairs)


def to_chip(x, by):
    devices = lax.axis_size("group")
    return lax.ppermute(x, "group", [(i, (i + 2 * by) % devices) for i in range(devices)])


def to_core(x):
    return lax.ppermute(x, "group", [(i, i ^ 1) for i in range(lax.axis_size("group"))])


def body(object_field, probe, amplitudes, row_offset, col_offset, counts):
    parts = lax.axis_size("group")
    index = lax.axis_index("group")
    group = index[None]
    rows, size = object_field.shape[1:]
    slots = amplitudes.shape[0]
    kept = rows // parts
    blocks = object_field.reshape(2, kept // SUB, parts, SUB, size)

    def share(which):
        return lax.dynamic_index_in_dim(blocks, which, 2, keepdims=False)

    mine = share(index)
    near = passed_along(mine, "tile", -1)
    near, opposite = lax.optimization_barrier((near, share((index + 4) % parts)))
    opposite = passed_along(opposite, "tile", -1)
    before, after = to_chip(near, 1), to_chip(near, -1)
    pieces = []
    for piece in (near, before, after, opposite):
        pieces += [piece, to_core(piece)]
    sent = patterns(group, object_field, pieces, probe, amplitudes, row_offset, col_offset, counts)
    got = lax.all_to_all(sent, "group", 0, 0)
    notes = got[:, slots * 2 * (size // parts), : 2 * slots + 1].astype(jnp.int32)
    notes_before = passed_along(notes, "tile", 1)
    here, spill = gathered(group, notes, got, slots, kept)
    spill = passed_along(spill, "tile", 1)
    weight = illumination(group, notes, notes_before, probe, slots, kept)
    result = mine + ((here + spill) / weight).reshape(mine.shape)
    before, after = to_chip(result, 1), to_chip(result, -1)
    upper, lower = to_chip(before[0], 1), to_chip(after[1], -1)
    pieces = []
    for piece in (result, before, after, upper, lower):
        pieces += [piece, to_core(piece)]
    return assembled(group, pieces, blocks.shape).reshape(object_field.shape)


def solution(mesh):
    in_specs = (
        P(None, None, "tile"),
        P(),
        P(("tile", "group"), None, None),
        P(("tile", "group")),
        P(("tile", "group")),
        P(("tile", "group")),
    )
    out_specs = P(None, None, "tile")
    return jax.shard_map(body, mesh=mesh, in_specs=in_specs, out_specs=out_specs, check_vma=False)
```

```python
import functools
import math

import jax
import jax.numpy as jnp
import numpy as np
from jax import lax
from jax.experimental import pallas as pl
from jax.experimental.pallas import tpu as pltpu
from jax.sharding import PartitionSpec as P

FLOOR = 0.25
REG = 0.5
SUB = 8
MIB = 2**20

STEPS = (0, -2, 2, 4)


def tables(length):
    steps = np.arange(length)
    angle = (steps[:, None] * steps[None, :] % length) * (2.0 * math.pi / length)
    factor = 1.0 / math.sqrt(length)
    cos, sin = np.cos(angle) * factor, np.sin(angle) * factor
    parts = []
    for table in (cos, cos - sin, cos + sin):
        table = table.astype(np.float32)
        high = table.astype(jnp.bfloat16)
        low = (table - high.astype(np.float32)).astype(jnp.bfloat16)
        parts += [high, low]
    return np.stack(parts)


def split(x):
    high = x.astype(jnp.bfloat16)
    return high, (x - high.astype(jnp.float32)).astype(jnp.bfloat16)


def dot(a, b):
    return jnp.dot(a, b, preferred_element_type=jnp.float32)


def right(x, tab, which):
    high, low = split(x)
    th, tl = tab[2 * which], tab[2 * which + 1]
    return dot(high, th) + dot(low, th) + dot(high, tl)


def left(x, tab, which):
    high, low = split(x)
    th, tl = tab[2 * which], tab[2 * which + 1]
    return dot(th, high) + dot(th, low) + dot(tl, high)


def forward(mul, a, b, tab):
    both = mul(a + b, tab, 0)
    return both - mul(b, tab, 1), both - mul(a, tab, 2)


def inverse(mul, a, b, tab):
    both = mul(a + b, tab, 0)
    return both - mul(b, tab, 2), both - mul(a, tab, 1)


def class_of(group, step, other, parts):
    index = (group + step) & (parts - 1)
    return index ^ 1 if other else index


def patterns_kernel(size, rows, parts, slots, notes_ref, own_ref, probe_hbm, amp_hbm, tab_hbm, held_ref, swapped_ref, out_ref,
                    own_buf, rim_buf, probe_ref, amp_ref, tab_ref, stage, own_sems, fixed_sems, piece_sems, store_sems):
    count, group = notes_ref[0, 2 * slots], notes_ref[2, 0]
    span = size + SUB
    depth = size // parts

    def start_of(p):
        return pl.multiple_of(notes_ref[0, p] & -SUB, SUB)

    def first_of(p):
        return pl.multiple_of(jnp.minimum(start_of(p), rows - span), SUB)

    def load(p):
        slot = lax.rem(p, 2)
        return pltpu.make_async_copy(own_ref.at[:, pl.ds(first_of(p), span)], own_buf.at[slot], own_sems.at[slot])

    def store(p):
        where = pl.ds(pl.multiple_of(p * 2 * depth, 2 * depth), 2 * depth)
        return pltpu.make_async_copy(stage.at[:, where], out_ref.at[:, where], store_sems.at[p])

    fixed = [
        pltpu.make_async_copy(a, b, fixed_sems.at[n])
        for n, (a, b) in enumerate(((probe_hbm, probe_ref), (tab_hbm, tab_ref), (amp_hbm, amp_ref)))
    ]
    rims = []
    for other, ref in enumerate((held_ref, swapped_ref)):
        for n, step in enumerate(STEPS):
            index = class_of(group, step, other, parts)
            rims.append(pltpu.make_async_copy(ref.at[n], rim_buf.at[:, :, index], piece_sems.at[len(rims)]))
    load(0).start()
    for copy in rims + fixed:
        copy.start()

    lane = lax.broadcasted_iota(jnp.int32, (SUB, size), 1)
    head_row = lax.broadcasted_iota(jnp.int32, (SUB, size), 0)
    column = lax.broadcasted_iota(jnp.int32, (size, size), 1)
    note = jnp.zeros((SUB, size), jnp.int32)
    for side in range(2):
        for n in range(2 * slots + 1):
            note = jnp.where(jnp.logical_and(head_row == side, lane == n), notes_ref[side, n], note)
    note = note.astype(jnp.float32)
    for part in range(parts):
        stage[part, slots * 2 * depth :] = note
    notes = pl.ds(slots * 2 * depth, SUB)
    last = pltpu.make_async_copy(stage.at[:, notes], out_ref.at[:, notes], store_sems.at[slots])
    last.start()
    for copy in fixed + rims:
        copy.wait()
    rim = rim_buf.reshape(2, rows, size)

    def pattern(p, _):
        slot = lax.rem(p, 2)
        row, col = notes_ref[0, p], notes_ref[0, slots + p]
        base = start_of(p)
        shift = row - base

        @pl.when(p + 1 < count)
        def _():
            load(p + 1).start()

        pr, pi = [pltpu.roll(pltpu.roll(probe_ref[ch], shift, 0), col, 1) for ch in range(2)]
        mine = column >= col
        load(p).wait()
        lead = pl.multiple_of(base - first_of(p), SUB)
        tail = pl.multiple_of(jnp.minimum(lead + size, size), SUB)
        tail_rim = pl.multiple_of(jnp.minimum(base + size, rows - SUB), SUB)

        def window(ch):
            full = jnp.where(mine, own_buf[slot, ch, pl.ds(lead, size)], rim[ch, pl.ds(base, size)])
            wrap = jnp.where(mine[:SUB], own_buf[slot, ch, pl.ds(tail, SUB)], rim[ch, pl.ds(tail_rim, SUB)])
            head = jnp.where(head_row >= shift, full[:SUB], wrap)
            return jnp.concatenate([head, full[SUB:]], axis=0)

        o_re, o_im = window(0), window(1)
        a = pr * o_re - pi * o_im
        b = pr * o_im + pi * o_re
        a, b = forward(right, a, b, tab_ref)
        a, b = forward(left, a, b, tab_ref)
        factor = amp_ref[p].astype(jnp.float32) * lax.rsqrt(jnp.maximum(a * a + b * b, FLOOR * FLOOR)) - 1.0
        a, b = a * factor, b * factor
        a, b = inverse(left, a, b, tab_ref)
        a, b = inverse(right, a, b, tab_ref)
        for ch, g in enumerate((pr * a + pi * b, pr * b - pi * a)):
            for t in range(parts):
                index = ((base >> 3) + t) & (parts - 1)
                for m in range(depth // SUB):
                    at = pl.multiple_of((2 * p + ch) * depth + SUB * m, SUB)
                    block = SUB * (parts * m + t)
                    stage[index, pl.ds(at, SUB)] = g[block : block + SUB]
        store(p).start()
        return 0

    lax.fori_loop(0, count, pattern, 0)

    def stored(p, _):
        store(p).wait()
        return 0

    last.wait()
    lax.fori_loop(0, count, stored, 0)


def patterns(notes, own, held, swapped, probe, amplitudes):
    rows, size = own.shape[1:]
    slots, parts = amplitudes.shape[0], 2 * held.shape[0]
    depth = size // parts
    length = slots * 2 * depth + SUB
    smem = pl.BlockSpec(memory_space=pltpu.SMEM)
    anywhere = pl.BlockSpec(memory_space=pl.ANY)
    hbm = pl.BlockSpec(memory_space=pltpu.HBM)
    tab = jnp.asarray(tables(size))
    return pl.pallas_call(
        functools.partial(patterns_kernel, size, rows, parts, slots),
        out_shape=jax.ShapeDtypeStruct((parts, length, size), jnp.float32),
        in_specs=[smem] + [hbm] * 4 + [anywhere] * 2,
        out_specs=anywhere,
        scratch_shapes=[
            pltpu.VMEM((2, 2, size + SUB, size), jnp.float32),
            pltpu.VMEM((2, rows // (SUB * parts), parts, SUB, size), jnp.float32),
            pltpu.VMEM(probe.shape, jnp.float32),
            pltpu.VMEM(amplitudes.shape, amplitudes.dtype),
            pltpu.VMEM(tab.shape, tab.dtype),
            pltpu.VMEM((parts, length, size), jnp.float32),
            pltpu.SemaphoreType.DMA((2,)),
            pltpu.SemaphoreType.DMA((3,)),
            pltpu.SemaphoreType.DMA((parts,)),
            pltpu.SemaphoreType.DMA((slots + 1,)),
        ],
        compiler_params=pltpu.CompilerParams(vmem_limit_bytes=40 * MIB),
        cost_estimate=pl.CostEstimate(flops=36 * 2 * size**3 * slots, bytes_accessed=12 * MIB, transcendentals=0),
        name="patterns",
    )(notes, own, probe, amplitudes, tab, held, swapped)


def place(row, group, parts):
    block = row >> 3
    first = (group - block) & (parts - 1)
    local = (block + first - group) >> (parts.bit_length() - 1)
    return first, pl.multiple_of(local * SUB, SUB), jnp.where(first == 0, row & (SUB - 1), 0)


def each_live(notes_ref, slots, step):
    def device(d, _):
        def pattern(p, _):
            step(d, p, notes_ref[d, p], notes_ref[d, slots + p])
            return 0

        return lax.fori_loop(0, notes_ref[d, 2 * slots], pattern, 0)

    lax.fori_loop(0, notes_ref.shape[0], device, 0)


def gather_kernel(size, parts, slots, group_ref, notes_ref, got_ref, here_ref, next_re_ref, next_im_ref, total):
    depth = size // parts
    group = group_ref[0]
    total[...] = jnp.zeros_like(total)
    column = lax.broadcasted_iota(jnp.int32, (depth, size), 1)
    head_row = lax.broadcasted_iota(jnp.int32, (SUB, size), 0)

    def step(d, p, row, col):
        _, at, shift = place(row, group, parts)
        mine = column >= col
        for ch in range(2):
            block = got_ref[d, pl.ds(pl.multiple_of((2 * p + ch) * depth, depth), depth)]
            for side in range(2):
                part = jnp.where(mine if side == 0 else jnp.logical_not(mine), block, 0.0)
                head = part[:SUB]
                total[side, ch, pl.ds(at, SUB)] += jnp.where(head_row >= shift, head, 0.0)
                total[side, ch, pl.ds(at + SUB, depth - SUB)] += part[SUB:]
                total[side, ch, pl.ds(at + depth, SUB)] += jnp.where(head_row < shift, head, 0.0)

    each_live(notes_ref, slots, step)
    kept = here_ref.shape[1]
    here_ref[...] = total[0, :, :kept]
    next_re_ref[...] = total[1, 0, :kept]
    next_im_ref[...] = total[1, 1, :kept]


def gathered(group, notes, got, slots, kept):
    parts, length, size = got.shape
    smem = pl.BlockSpec(memory_space=pltpu.SMEM)
    vmem = pl.BlockSpec(memory_space=pltpu.VMEM)
    shape = jax.ShapeDtypeStruct((kept, size), jnp.float32)
    both = jax.ShapeDtypeStruct((2, kept, size), jnp.float32)
    return pl.pallas_call(
        functools.partial(gather_kernel, size, parts, slots),
        out_shape=(both, shape, shape),
        in_specs=[smem, smem, vmem],
        out_specs=(vmem, vmem, vmem),
        scratch_shapes=[pltpu.VMEM((2, 2, kept + SUB, size), jnp.float32)],
        compiler_params=pltpu.CompilerParams(vmem_limit_bytes=24 * MIB),
        cost_estimate=pl.CostEstimate(flops=2**22, bytes_accessed=6 * MIB, transcendentals=0),
        name="gathered",
    )(group, notes, got)


def illumination_kernel(size, parts, slots, group_ref, here_ref, before_ref, probe_ref, out_ref, intensity, total):
    depth = size // parts
    group = group_ref[0]
    square = probe_ref[0] * probe_ref[0] + probe_ref[1] * probe_ref[1]
    intensity[:SUB] = square[size - SUB :]
    intensity[SUB:] = square
    total[...] = jnp.zeros_like(total)
    column = lax.broadcasted_iota(jnp.int32, (depth, size), 1)
    head_row = lax.broadcasted_iota(jnp.int32, (SUB, size), 0)

    for side, ref in enumerate((here_ref, before_ref)):

        def step(d, p, row, col):
            first, at, shift = place(row, group, parts)
            down = row & (SUB - 1)
            blocks = []
            for m in range(depth // SUB):
                start = pl.multiple_of((parts * m + first) * SUB, SUB)
                above, below = [pltpu.roll(intensity[pl.ds(start + n * SUB, SUB)], down, 0) for n in range(2)]
                blocks.append(jnp.where(head_row >= down, below, above))
            placed = pltpu.roll(jnp.concatenate(blocks, axis=0), col, 1)
            part = jnp.where(column >= col if side == 0 else column < col, placed, 0.0)
            head = part[:SUB]
            total[pl.ds(at, SUB)] += jnp.where(head_row >= shift, head, 0.0)
            total[pl.ds(at + SUB, depth - SUB)] += part[SUB:]
            total[pl.ds(at + depth, SUB)] += jnp.where(head_row < shift, head, 0.0)

        each_live(ref, slots, step)
    out_ref[...] = total[: out_ref.shape[0]] + REG


def illumination(group, here, before, probe, slots, kept):
    size = probe.shape[1]
    parts = here.shape[0]
    smem = pl.BlockSpec(memory_space=pltpu.SMEM)
    vmem = pl.BlockSpec(memory_space=pltpu.VMEM)
    return pl.pallas_call(
        functools.partial(illumination_kernel, size, parts, slots),
        out_shape=jax.ShapeDtypeStruct((kept, size), jnp.float32),
        in_specs=[smem, smem, smem, vmem],
        out_specs=vmem,
        scratch_shapes=[
            pltpu.VMEM((size + SUB, size), jnp.float32),
            pltpu.VMEM((kept + SUB, size), jnp.float32),
        ],
        compiler_params=pltpu.CompilerParams(vmem_limit_bytes=16 * MIB),
        cost_estimate=pl.CostEstimate(flops=2**22, bytes_accessed=8 * MIB, transcendentals=0),
        name="illumination",
    )(group, here, before, probe)


def assemble_kernel(steps, parts, group_ref, held_ref, swapped_ref, *refs):
    out_ref, sems = refs[-2:]
    copies = []
    for other, ref in enumerate((held_ref, swapped_ref)):
        for n, step in enumerate(steps):
            index = class_of(group_ref[0], step, other, parts)
            copies.append(pltpu.make_async_copy(ref.at[n], out_ref.at[n % 2, :, index], sems.at[len(copies)]))
    for copy in copies:
        copy.start()
    for copy in copies:
        copy.wait()


def assembled(group, steps, held, swapped, shape, begun=()):
    parts = shape[2]
    hbm = pl.BlockSpec(memory_space=pltpu.HBM)
    vmem = pl.BlockSpec(memory_space=pltpu.VMEM)
    return pl.pallas_call(
        functools.partial(assemble_kernel, steps, parts),
        out_shape=jax.ShapeDtypeStruct(shape, jnp.float32),
        in_specs=[pl.BlockSpec(memory_space=pltpu.SMEM), vmem, vmem] + [hbm] * len(begun),
        out_specs=hbm,
        scratch_shapes=[pltpu.SemaphoreType.DMA((2 * len(steps),))],
        input_output_aliases={3: 0} if begun else {},
        cost_estimate=pl.CostEstimate(flops=0, bytes_accessed=8 * MIB, transcendentals=0),
        name="assembled",
    )(group, held, swapped, *begun)


def passed_along(x, axis, by):
    devices = lax.axis_size(axis)
    pairs = [(i, i + by) for i in range(devices) if 0 <= i + by < devices]
    return lax.ppermute(x, axis, pairs)


def to_chip(x, by):
    devices = lax.axis_size("group")
    return lax.ppermute(x, "group", [(i, (i + 2 * by) % devices) for i in range(devices)])


def to_core(x):
    return lax.ppermute(x, "group", [(i, i ^ 1) for i in range(lax.axis_size("group"))])


def body(object_field, probe, amplitudes, row_offset, col_offset, counts):
    parts = lax.axis_size("group")
    index = lax.axis_index("group")
    group = index[None]
    rows, size = object_field.shape[1:]
    slots = amplitudes.shape[0]
    kept = rows // parts
    blocks = object_field.reshape(2, kept // SUB, parts, SUB, size)

    def share(which):
        return lax.dynamic_index_in_dim(blocks, which, 2, keepdims=False)

    mine = share(index)
    near = passed_along(mine, "tile", -1)
    near, opposite = lax.optimization_barrier((near, share((index + 4) % parts)))
    opposite = passed_along(opposite, "tile", -1)
    held = jnp.stack([near, to_chip(near, 1), to_chip(near, -1), opposite])
    own_notes = jnp.concatenate([row_offset, col_offset, counts])
    notes = jnp.stack([own_notes, passed_along(own_notes, "tile", 1), jnp.full_like(own_notes, index)])
    sent = patterns(notes, object_field, held, to_core(held), probe, amplitudes)
    got = lax.all_to_all(sent, "group", 0, 0)
    notes = got[:, slots * 2 * (size // parts) :, : 2 * slots + 1].astype(jnp.int32)
    notes_here, notes_before = notes[:, 0], notes[:, 1]
    here, *spills = gathered(group, notes_here, got, slots, kept)
    weight = illumination(group, notes_here, notes_before, probe, slots, kept)
    results, before, after = [], [], []
    for ch, spill in enumerate(spills):
        grad = here[ch] + passed_along(spill, "tile", 1)
        results.append(mine[ch] + (grad / weight).reshape(mine.shape[1:]))
        before.append(to_chip(results[ch], 1))
        after.append(to_chip(results[ch], -1))
    first = jnp.stack(results + before + after)
    last = jnp.stack([to_chip(before[0], 1), to_chip(after[1], -1)])
    field = assembled(group, (0, 0, -2, -2, 2, 2), first, to_core(first), blocks.shape)
    field = assembled(group, (4, 4), last, to_core(last), blocks.shape, (field,))
    return field.reshape(object_field.shape)


def solution(mesh):
    in_specs = (
        P(None, None, "tile"),
        P(),
        P(("tile", "group"), None, None),
        P(("tile", "group")),
        P(("tile", "group")),
        P(("tile", "group")),
    )
    out_specs = P(None, None, "tile")
    return jax.shard_map(body, mesh=mesh, in_specs=in_specs, out_specs=out_specs, check_vma=False)
```

```python
import functools
import math

import jax
import jax.numpy as jnp
import numpy as np
from jax import lax
from jax.experimental import pallas as pl
from jax.experimental.pallas import tpu as pltpu
from jax.sharding import PartitionSpec as P

FLOOR = 0.25
REG = 0.5
SUB = 8
MIB = 2**20

STEPS = (0, -2, 2, 4)


def tables(length):
    half = length // 2
    place, freq = np.arange(half)[:, None], np.arange(half)[None, :]
    scale = 1.0 / math.sqrt(length)
    even, odd = [], []
    for parity, out in ((0, even), (1, odd)):
        angle = (place * (2 * freq + parity) % length) * (2.0 * math.pi / length)
        cos, sin = np.cos(angle) * scale, np.sin(angle) * scale
        by_place = np.block([[cos, -sin], [sin, cos]])
        out += [by_place, by_place.T, by_place, by_place.T]
    parts = []
    for table in [table for pair in zip(even, odd) for table in pair]:
        table = table.astype(np.float32)
        high = table.astype(jnp.bfloat16)
        parts += [high, (table - high.astype(np.float32)).astype(jnp.bfloat16)]
    return np.stack(parts)


def split(x):
    high = x.astype(jnp.bfloat16)
    return high, (x - high.astype(jnp.float32)).astype(jnp.bfloat16)


def dot(a, b):
    return jnp.dot(a, b, preferred_element_type=jnp.float32)


def right(x, high_tab, low_tab):
    high, low = split(x)
    return dot(high, high_tab) + dot(low, high_tab) + dot(high, low_tab)


def left(x, high_tab, low_tab):
    high, low = split(x)
    return dot(high_tab, high) + dot(high_tab, low) + dot(low_tab, high)


def halves(x, axis):
    half = x.shape[axis] // 2
    return lax.slice_in_dim(x, 0, half, axis=axis), lax.slice_in_dim(x, half, 2 * half, axis=axis)


def join(parts, axis):
    return jnp.concatenate(parts, axis=axis)


def forward(mul, axis, a, b, tabs):
    (a0, a1), (b0, b1) = halves(a, axis), halves(b, axis)
    even = mul(join([a0 + a1, b0 + b1], axis), tabs[0], tabs[1])
    odd = mul(join([a0 - a1, b0 - b1], axis), tabs[2], tabs[3])
    (a0, b0), (a1, b1) = halves(even, axis), halves(odd, axis)
    return join([a0, a1], axis), join([b0, b1], axis)


def inverse(mul, axis, a, b, tabs):
    (a0, a1), (b0, b1) = halves(a, axis), halves(b, axis)
    even = mul(join([a0, b0], axis), tabs[0], tabs[1])
    odd = mul(join([a1, b1], axis), tabs[2], tabs[3])
    (a0, b0), (a1, b1) = halves(even, axis), halves(odd, axis)
    return join([a0 + a1, a0 - a1], axis), join([b0 + b1, b0 - b1], axis)


def class_of(group, step, other, parts):
    index = (group + step) & (parts - 1)
    return index ^ 1 if other else index


def patterns_kernel(size, rows, parts, slots, notes_ref, own_ref, probe_hbm, amp_hbm, tab_hbm, held_ref, other_ref, out_ref,
                    own_buf, rim_buf, probe_ref, amp_ref, tab_ref, stage, own_sems, fixed_sems, piece_sems, store_sems):
    count, group = notes_ref[0, 2 * slots], notes_ref[2, 0]
    span = size + SUB
    depth = size // parts

    def start_of(p):
        return pl.multiple_of(notes_ref[0, p] & -SUB, SUB)

    def first_of(p):
        return pl.multiple_of(jnp.minimum(start_of(p), rows - span), SUB)

    def loads(p):
        slot = 2 * lax.rem(p >> 1, 2)
        return [
            pltpu.make_async_copy(
                own_ref.at[:, pl.ds(first_of(jnp.minimum(p + n, count - 1)), span)], own_buf.at[slot + n], own_sems.at[slot + n])
            for n in range(2)
        ]

    def store(p):
        where = pl.ds(pl.multiple_of(p * 4 * depth, 4 * depth), 4 * depth)
        return pltpu.make_async_copy(stage.at[:, where], out_ref.at[:, where], store_sems.at[p])

    fixed = [
        pltpu.make_async_copy(a, b, fixed_sems.at[n])
        for n, (a, b) in enumerate(((probe_hbm, probe_ref), (tab_hbm, tab_ref), (amp_hbm, amp_ref)))
    ]
    rims = []
    for other, ref in enumerate((held_ref, other_ref)):
        for n, step in enumerate(STEPS):
            index = class_of(group, step, other, parts)
            rims.append(pltpu.make_async_copy(ref.at[n], rim_buf.at[:, :, index], piece_sems.at[len(rims)]))
    for copy in loads(0) + rims + fixed:
        copy.start()

    lane = lax.broadcasted_iota(jnp.int32, (SUB, size), 1)
    head_row = lax.broadcasted_iota(jnp.int32, (SUB, size), 0)
    column = lax.broadcasted_iota(jnp.int32, (size, size), 1)
    note = jnp.zeros((SUB, size), jnp.int32)
    for side in range(2):
        for n in range(2 * slots + 1):
            note = jnp.where(jnp.logical_and(head_row == side, lane == n), notes_ref[side, n], note)
    note = note.astype(jnp.float32)
    for part in range(parts):
        stage[part, slots * 2 * depth :] = note
    notes = pl.ds(slots * 2 * depth, SUB)
    last = pltpu.make_async_copy(stage.at[:, notes], out_ref.at[:, notes], store_sems.at[slots])
    last.start()
    for copy in fixed + rims:
        copy.wait()
    rim = rim_buf.reshape(2, rows, size)

    def moved_down(ref, shift):
        blocks = [pltpu.roll(ref[SUB * n : SUB * (n + 1)], shift, 0) for n in range(size // SUB)]
        return jnp.concatenate([jnp.where(head_row >= shift, here, above) for here, above in zip(blocks, blocks[-1:] + blocks)], axis=0)

    def prepare(p, slot):
        row, col = notes_ref[0, p], notes_ref[0, slots + p]
        base = start_of(p)
        shift = row - base
        pr, pi = [pltpu.roll(moved_down(probe_ref.at[ch], shift), col, 1) for ch in range(2)]
        mine = column >= col
        lead = pl.multiple_of(base - first_of(p), SUB)
        tail = pl.multiple_of(jnp.minimum(lead + size, size), SUB)
        tail_rim = pl.multiple_of(jnp.minimum(base + size, rows - SUB), SUB)

        def window(ch):
            full = jnp.where(mine, own_buf[slot, ch, pl.ds(lead, size)], rim[ch, pl.ds(base, size)])
            wrap = jnp.where(mine[:SUB], own_buf[slot, ch, pl.ds(tail, SUB)], rim[ch, pl.ds(tail_rim, SUB)])
            head = jnp.where(head_row >= shift, full[:SUB], wrap)
            return jnp.concatenate([head, full[SUB:]], axis=0)

        o_re, o_im = window(0), window(1)
        return base, pr, pi, pr * o_re - pi * o_im, pr * o_im + pi * o_re

    def constrain(p, a, b):
        factor = amp_ref[p].astype(jnp.float32) * lax.rsqrt(jnp.maximum(a * a + b * b, FLOOR * FLOOR)) - 1.0
        return a * factor, b * factor

    def put(p, base, pr, pi, a, b):
        for ch, g in enumerate((pr * a + pi * b, pr * b - pi * a)):
            for t in range(parts):
                index = ((base >> 3) + t) & (parts - 1)
                for m in range(depth // SUB):
                    at = pl.multiple_of((2 * p + ch) * depth + SUB * m, SUB)
                    block = SUB * (parts * m + t)
                    stage[index, pl.ds(at, SUB)] = g[block : block + SUB]

    def pair(n, _):
        first = 2 * n
        second = jnp.minimum(first + 1, count - 1)

        @pl.when(first + 2 < count)
        def _():
            for copy in loads(first + 2):
                copy.start()

        for copy in loads(first):
            copy.wait()
        slot = 2 * lax.rem(n, 2)
        work = [(first, slot), (second, slot + 1)]
        states = [prepare(p, at) for p, at in work]
        waves = [state[3:] for state in states]
        tabs = [[tab_ref[4 * stage + n] for n in range(4)] for stage in range(4)]
        waves = [forward(right, 1, *wave, tabs[0]) for wave in waves]
        waves = [forward(left, 0, *wave, tabs[1]) for wave in waves]
        waves = [constrain(p, *wave) for (p, _), wave in zip(work, waves)]
        waves = [inverse(left, 0, *wave, tabs[2]) for wave in waves]
        waves = [inverse(right, 1, *wave, tabs[3]) for wave in waves]
        for (p, _), state, wave in zip(work, states, waves):
            put(p, *state[:3], *wave)
        store(n).start()
        return 0

    pairs = (count + 1) >> 1
    lax.fori_loop(0, pairs, pair, 0)

    def stored(p, _):
        store(p).wait()
        return 0

    last.wait()
    lax.fori_loop(0, pairs, stored, 0)


def ordered_kernel(order_ref, turned_ref, amp_ref, out_ref):
    order, turned = order_ref[...], turned_ref[...]
    for p in range(amp_ref.shape[0]):
        rows = dot(order, amp_ref[p]).astype(jnp.bfloat16)
        out_ref[p] = dot(rows, turned).astype(jnp.bfloat16)


def ordered(amplitudes):
    size = amplitudes.shape[1]
    order = np.zeros((size, size), np.float32)
    order[np.arange(size), np.concatenate([np.arange(0, size, 2), np.arange(1, size, 2)])] = 1.0
    vmem = pl.BlockSpec(memory_space=pltpu.VMEM)
    return pl.pallas_call(
        ordered_kernel,
        out_shape=jax.ShapeDtypeStruct(amplitudes.shape, amplitudes.dtype),
        in_specs=[vmem] * 3,
        out_specs=vmem,
        compiler_params=pltpu.CompilerParams(vmem_limit_bytes=16 * MIB),
        cost_estimate=pl.CostEstimate(flops=2**28, bytes_accessed=2 * MIB, transcendentals=0),
        name="ordered",
    )(jnp.asarray(order, jnp.bfloat16), jnp.asarray(order.T, jnp.bfloat16), amplitudes)


def patterns(notes, own, held, other, probe, amplitudes):
    rows, size = own.shape[1:]
    slots, parts = amplitudes.shape[0], 2 * len(STEPS)
    depth = size // parts
    length = slots * 2 * depth + SUB
    smem = pl.BlockSpec(memory_space=pltpu.SMEM)
    anywhere = pl.BlockSpec(memory_space=pl.ANY)
    hbm = pl.BlockSpec(memory_space=pltpu.HBM)
    tab = jnp.asarray(tables(size))
    return pl.pallas_call(
        functools.partial(patterns_kernel, size, rows, parts, slots),
        out_shape=jax.ShapeDtypeStruct((parts, length, size), jnp.float32),
        in_specs=[smem] + [hbm] * 4 + [anywhere] * 2,
        out_specs=anywhere,
        scratch_shapes=[
            pltpu.VMEM((4, 2, size + SUB, size), jnp.float32),
            pltpu.VMEM((2, rows // (SUB * parts), parts, SUB, size), jnp.float32),
            pltpu.VMEM(probe.shape, jnp.float32),
            pltpu.VMEM(amplitudes.shape, amplitudes.dtype),
            pltpu.VMEM(tab.shape, tab.dtype),
            pltpu.VMEM((parts, length, size), jnp.float32),
            pltpu.SemaphoreType.DMA((4,)),
            pltpu.SemaphoreType.DMA((3,)),
            pltpu.SemaphoreType.DMA((parts,)),
            pltpu.SemaphoreType.DMA((slots + 1,)),
        ],
        compiler_params=pltpu.CompilerParams(vmem_limit_bytes=40 * MIB),
        cost_estimate=pl.CostEstimate(flops=24 * 2 * size**3 * slots, bytes_accessed=12 * MIB, transcendentals=0),
        name="patterns",
    )(notes, own, probe, amplitudes, tab, held, other)


def place(row, group, parts):
    block = row >> 3
    first = (group - block) & (parts - 1)
    local = (block + first - group) >> (parts.bit_length() - 1)
    return first, pl.multiple_of(local * SUB, SUB), jnp.where(first == 0, row & (SUB - 1), 0)


def each_live(notes_ref, slots, step):
    def device(d, _):
        def pattern(p, _):
            step(d, p, notes_ref[d, p], notes_ref[d, slots + p])
            return 0

        return lax.fori_loop(0, notes_ref[d, 2 * slots], pattern, 0)

    lax.fori_loop(0, notes_ref.shape[0], device, 0)


def gather_kernel(size, parts, slots, group_ref, notes_ref, got_ref, here_ref, next_ref, total):
    depth = size // parts
    group = group_ref[0]
    total[...] = jnp.zeros_like(total)
    column = lax.broadcasted_iota(jnp.int32, (depth, size), 1)
    head_row = lax.broadcasted_iota(jnp.int32, (SUB, size), 0)

    def step(d, p, row, col):
        _, at, shift = place(row, group, parts)
        mine = column >= col
        for ch in range(2):
            block = got_ref[d, pl.ds(pl.multiple_of((2 * p + ch) * depth, depth), depth)]
            for side in range(2):
                part = jnp.where(mine if side == 0 else jnp.logical_not(mine), block, 0.0)
                head = part[:SUB]
                total[side, ch, pl.ds(at, SUB)] += jnp.where(head_row >= shift, head, 0.0)
                total[side, ch, pl.ds(at + SUB, depth - SUB)] += part[SUB:]
                total[side, ch, pl.ds(at + depth, SUB)] += jnp.where(head_row < shift, head, 0.0)

    each_live(notes_ref, slots, step)
    kept = here_ref.shape[1]
    here_ref[...] = total[0, :, :kept]
    next_ref[...] = total[1, :, :kept]


def gathered(group, notes, got, slots, kept):
    parts, length, size = got.shape
    smem = pl.BlockSpec(memory_space=pltpu.SMEM)
    vmem = pl.BlockSpec(memory_space=pltpu.VMEM)
    shape = jax.ShapeDtypeStruct((2, kept, size), jnp.float32)
    return pl.pallas_call(
        functools.partial(gather_kernel, size, parts, slots),
        out_shape=(shape, shape),
        in_specs=[smem, smem, vmem],
        out_specs=(vmem, vmem),
        scratch_shapes=[pltpu.VMEM((2, 2, kept + SUB, size), jnp.float32)],
        compiler_params=pltpu.CompilerParams(vmem_limit_bytes=24 * MIB),
        cost_estimate=pl.CostEstimate(flops=2**22, bytes_accessed=6 * MIB, transcendentals=0),
        name="gathered",
    )(group, notes, got)


def illumination_kernel(size, parts, slots, group_ref, here_ref, before_ref, probe_ref, out_ref, intensity, total):
    depth = size // parts
    group = group_ref[0]
    square = probe_ref[0] * probe_ref[0] + probe_ref[1] * probe_ref[1]
    intensity[:SUB] = square[size - SUB :]
    intensity[SUB:] = square
    total[...] = jnp.zeros_like(total)
    column = lax.broadcasted_iota(jnp.int32, (depth, size), 1)
    head_row = lax.broadcasted_iota(jnp.int32, (SUB, size), 0)

    for side, ref in enumerate((here_ref, before_ref)):

        def step(d, p, row, col):
            first, at, shift = place(row, group, parts)
            down = row & (SUB - 1)
            blocks = []
            for m in range(depth // SUB):
                start = pl.multiple_of((parts * m + first) * SUB, SUB)
                above, below = [pltpu.roll(intensity[pl.ds(start + n * SUB, SUB)], down, 0) for n in range(2)]
                blocks.append(jnp.where(head_row >= down, below, above))
            placed = pltpu.roll(jnp.concatenate(blocks, axis=0), col, 1)
            part = jnp.where(column >= col if side == 0 else column < col, placed, 0.0)
            head = part[:SUB]
            total[pl.ds(at, SUB)] += jnp.where(head_row >= shift, head, 0.0)
            total[pl.ds(at + SUB, depth - SUB)] += part[SUB:]
            total[pl.ds(at + depth, SUB)] += jnp.where(head_row < shift, head, 0.0)

        each_live(ref, slots, step)
    out_ref[...] = total[: out_ref.shape[0]] + REG


def illumination(group, here, before, probe, slots, kept):
    size = probe.shape[1]
    parts = here.shape[0]
    smem = pl.BlockSpec(memory_space=pltpu.SMEM)
    vmem = pl.BlockSpec(memory_space=pltpu.VMEM)
    return pl.pallas_call(
        functools.partial(illumination_kernel, size, parts, slots),
        out_shape=jax.ShapeDtypeStruct((kept, size), jnp.float32),
        in_specs=[smem, smem, smem, vmem],
        out_specs=vmem,
        scratch_shapes=[
            pltpu.VMEM((size + SUB, size), jnp.float32),
            pltpu.VMEM((kept + SUB, size), jnp.float32),
        ],
        compiler_params=pltpu.CompilerParams(vmem_limit_bytes=16 * MIB),
        cost_estimate=pl.CostEstimate(flops=2**22, bytes_accessed=8 * MIB, transcendentals=0),
        name="illumination",
    )(group, here, before, probe)


def assemble_kernel(other, parts, group_ref, ref, *refs):
    out_ref, sems = refs[-2:]
    core = (group_ref[0] & 1) ^ other
    copies = [pltpu.make_async_copy(ref.at[n], out_ref.at[:, :, 2 * n + core], sems.at[n]) for n in range(parts // 2)]
    for copy in copies:
        copy.start()
    for copy in copies:
        copy.wait()


def assembled(group, other, shares, shape, begun=()):
    parts = shape[2]
    anywhere = pl.BlockSpec(memory_space=pl.ANY)
    hbm = pl.BlockSpec(memory_space=pltpu.HBM)
    return pl.pallas_call(
        functools.partial(assemble_kernel, other, parts),
        out_shape=jax.ShapeDtypeStruct(shape, jnp.float32),
        in_specs=[pl.BlockSpec(memory_space=pltpu.SMEM), anywhere] + [hbm] * len(begun),
        out_specs=hbm,
        scratch_shapes=[pltpu.SemaphoreType.DMA((parts // 2,))],
        input_output_aliases={2: 0} if begun else {},
        compiler_params=pltpu.CompilerParams(vmem_limit_bytes=MIB),
        cost_estimate=pl.CostEstimate(flops=0, bytes_accessed=4 * MIB, transcendentals=0),
        name="assembled",
    )(group, shares, *begun)


def passed_along(x, axis, by):
    devices = lax.axis_size(axis)
    pairs = [(i, i + by) for i in range(devices) if 0 <= i + by < devices]
    return lax.ppermute(x, axis, pairs)


def to_chip(x, by):
    devices = lax.axis_size("group")
    return lax.ppermute(x, "group", [(i, (i + 2 * by) % devices) for i in range(devices)])


def to_core(x):
    return lax.ppermute(x, "group", [(i, i ^ 1) for i in range(lax.axis_size("group"))])


def body(object_field, probe, amplitudes, row_offset, col_offset, counts):
    parts = lax.axis_size("group")
    index = lax.axis_index("group")
    group = index[None]
    rows, size = object_field.shape[1:]
    slots = amplitudes.shape[0]
    kept = rows // parts
    blocks = object_field.reshape(2, kept // SUB, parts, SUB, size)

    def share(which):
        return lax.dynamic_index_in_dim(blocks, which, 2, keepdims=False)

    mine = share(index)
    own_notes = jnp.concatenate([row_offset, col_offset, counts])
    near, opposite, notes_before = lax.optimization_barrier(
        (passed_along(mine, "tile", -1), share((index + 4) % parts), passed_along(own_notes, "tile", 1)))
    held = jnp.stack([near, to_chip(near, 1), to_chip(near, -1), passed_along(opposite, "tile", -1)])
    notes = jnp.stack([own_notes, notes_before, jnp.full_like(own_notes, index)])
    sent = patterns(notes, object_field, held, to_core(held), probe, ordered(amplitudes))
    got = lax.all_to_all(sent, "group", 0, 0)
    notes = got[:, slots * 2 * (size // parts) :, : 2 * slots + 1].astype(jnp.int32)
    notes_here, notes_before = notes[:, 0], notes[:, 1]
    here, spill = gathered(group, notes_here, got, slots, kept)
    spill = passed_along(spill, "tile", 1)
    weight = illumination(group, notes_here, notes_before, probe, slots, kept)
    result = mine + ((here + spill) / weight).reshape(mine.shape)
    chips = parts // 2
    same_core = [list(range(core, parts, 2)) for core in range(2)]
    spread = jnp.broadcast_to(result, (chips, *result.shape))
    shares = lax.all_to_all(spread, "group", 0, 0, axis_index_groups=same_core)
    field = assembled(group, 0, shares, blocks.shape)
    field = assembled(group, 1, to_core(shares), blocks.shape, (field,))
    return field.reshape(object_field.shape)


def solution(mesh):
    in_specs = (
        P(None, None, "tile"),
        P(),
        P(("tile", "group"), None, None),
        P(("tile", "group")),
        P(("tile", "group")),
        P(("tile", "group")),
    )
    out_specs = P(None, None, "tile")
    return jax.shard_map(body, mesh=mesh, in_specs=in_specs, out_specs=out_specs, check_vma=False)
```

```python
import functools
import math

import jax
import jax.numpy as jnp
import numpy as np
from jax import lax
from jax.experimental import pallas as pl
from jax.experimental.pallas import tpu as pltpu
from jax.sharding import PartitionSpec as P

FLOOR = 0.25
REG = 0.5
SUB = 8
MIB = 2**20

STEPS = (0, -2, 4, 2)


def tables(length):
    half = length // 2
    place, freq = np.arange(half)[:, None], np.arange(half)[None, :]
    scale = 1.0 / math.sqrt(length)
    even, odd = [], []
    for parity, out in ((0, even), (1, odd)):
        angle = (place * (2 * freq + parity) % length) * (2.0 * math.pi / length)
        cos, sin = np.cos(angle) * scale, np.sin(angle) * scale
        by_place = np.block([[cos, -sin], [sin, cos]])
        out += [by_place, by_place.T, by_place, by_place.T]
    parts = []
    for table in [table for pair in zip(even, odd) for table in pair]:
        table = table.astype(np.float32)
        high = table.astype(jnp.bfloat16)
        parts += [high, (table - high.astype(np.float32)).astype(jnp.bfloat16)]
    return np.stack(parts)


def split(x):
    high = x.astype(jnp.bfloat16)
    return high, (x - high.astype(jnp.float32)).astype(jnp.bfloat16)


def dot(a, b):
    return jnp.dot(a, b, preferred_element_type=jnp.float32)


def right(x, high_tab, low_tab):
    high, low = split(x)
    return dot(high, high_tab) + dot(low, high_tab) + dot(high, low_tab)


def left(x, high_tab, low_tab):
    high, low = split(x)
    return dot(high_tab, high) + dot(high_tab, low) + dot(low_tab, high)


def halves(x, axis):
    half = x.shape[axis] // 2
    return lax.slice_in_dim(x, 0, half, axis=axis), lax.slice_in_dim(x, half, 2 * half, axis=axis)


def join(parts, axis):
    return jnp.concatenate(parts, axis=axis)


def forward(mul, axis, a, b, tabs):
    (a0, a1), (b0, b1) = halves(a, axis), halves(b, axis)
    even = mul(join([a0 + a1, b0 + b1], axis), tabs[0], tabs[1])
    odd = mul(join([a0 - a1, b0 - b1], axis), tabs[2], tabs[3])
    (a0, b0), (a1, b1) = halves(even, axis), halves(odd, axis)
    return join([a0, a1], axis), join([b0, b1], axis)


def inverse(mul, axis, a, b, tabs):
    (a0, a1), (b0, b1) = halves(a, axis), halves(b, axis)
    even = mul(join([a0, b0], axis), tabs[0], tabs[1])
    odd = mul(join([a1, b1], axis), tabs[2], tabs[3])
    (a0, b0), (a1, b1) = halves(even, axis), halves(odd, axis)
    return join([a0 + a1, a0 - a1], axis), join([b0 + b1, b0 - b1], axis)


def class_of(group, step, other, parts):
    index = (group + step) & (parts - 1)
    return index ^ 1 if other else index


def patterns_kernel(size, rows, parts, slots, notes_ref, own_ref, probe_hbm, amp_hbm, tab_hbm, near_ref, far_ref, other_near_ref, other_far_ref, out_ref,
                    own_buf, rim_buf, probe_ref, amp_ref, tab_ref, stage, own_sems, fixed_sems, piece_sems, store_sems):
    count, group = notes_ref[0, 2 * slots], notes_ref[2, 0]
    span = size + SUB
    depth = size // parts

    def start_of(p):
        return pl.multiple_of(notes_ref[0, p] & -SUB, SUB)

    def first_of(p):
        return pl.multiple_of(jnp.minimum(start_of(p), rows - span), SUB)

    def loads(p):
        slot = 2 * lax.rem(p >> 1, 2)
        return [
            pltpu.make_async_copy(
                own_ref.at[:, pl.ds(first_of(jnp.minimum(p + n, count - 1)), span)], own_buf.at[slot + n], own_sems.at[slot + n])
            for n in range(2)
        ]

    def store(p):
        where = pl.ds(pl.multiple_of(p * 4 * depth, 4 * depth), 4 * depth)
        return pltpu.make_async_copy(stage.at[:, where], out_ref.at[:, where], store_sems.at[p])

    fixed = [
        pltpu.make_async_copy(a, b, fixed_sems.at[n])
        for n, (a, b) in enumerate(((probe_hbm, probe_ref), (tab_hbm, tab_ref), (amp_hbm, amp_ref)))
    ]
    rims = []
    for other, refs in enumerate(((near_ref, far_ref), (other_near_ref, other_far_ref))):
        for n, step in enumerate(STEPS):
            index = class_of(group, step, other, parts)
            rims.append(pltpu.make_async_copy(refs[n // 2].at[n % 2], rim_buf.at[:, :, index], piece_sems.at[len(rims)]))
    for copy in loads(0) + rims + fixed:
        copy.start()

    lane = lax.broadcasted_iota(jnp.int32, (SUB, size), 1)
    head_row = lax.broadcasted_iota(jnp.int32, (SUB, size), 0)
    column = lax.broadcasted_iota(jnp.int32, (size, size), 1)
    note = jnp.zeros((SUB, size), jnp.int32)
    for side in range(2):
        for n in range(2 * slots + 1):
            note = jnp.where(jnp.logical_and(head_row == side, lane == n), notes_ref[side, n], note)
    note = note.astype(jnp.float32)
    for part in range(parts):
        stage[part, slots * 2 * depth :] = note
    notes = pl.ds(slots * 2 * depth, SUB)
    last = pltpu.make_async_copy(stage.at[:, notes], out_ref.at[:, notes], store_sems.at[slots])
    last.start()
    for copy in fixed + rims:
        copy.wait()
    rim = rim_buf.reshape(2, rows, size)

    def moved_down(ref, shift):
        blocks = [pltpu.roll(ref[SUB * n : SUB * (n + 1)], shift, 0) for n in range(size // SUB)]
        return jnp.concatenate([jnp.where(head_row >= shift, here, above) for here, above in zip(blocks, blocks[-1:] + blocks)], axis=0)

    def prepare(p, slot):
        row, col = notes_ref[0, p], notes_ref[0, slots + p]
        base = start_of(p)
        shift = row - base
        pr, pi = [pltpu.roll(moved_down(probe_ref.at[ch], shift), col, 1) for ch in range(2)]
        mine = column >= col
        lead = pl.multiple_of(base - first_of(p), SUB)
        tail = pl.multiple_of(jnp.minimum(lead + size, size), SUB)
        tail_rim = pl.multiple_of(jnp.minimum(base + size, rows - SUB), SUB)

        def window(ch):
            full = jnp.where(mine, own_buf[slot, ch, pl.ds(lead, size)], rim[ch, pl.ds(base, size)])
            wrap = jnp.where(mine[:SUB], own_buf[slot, ch, pl.ds(tail, SUB)], rim[ch, pl.ds(tail_rim, SUB)])
            head = jnp.where(head_row >= shift, full[:SUB], wrap)
            return jnp.concatenate([head, full[SUB:]], axis=0)

        o_re, o_im = window(0), window(1)
        return base, pr, pi, pr * o_re - pi * o_im, pr * o_im + pi * o_re

    def constrain(p, a, b):
        factor = amp_ref[p].astype(jnp.float32) * lax.rsqrt(jnp.maximum(a * a + b * b, FLOOR * FLOOR)) - 1.0
        return a * factor, b * factor

    def put(p, base, pr, pi, a, b):
        for ch, g in enumerate((pr * a + pi * b, pr * b - pi * a)):
            for t in range(parts):
                index = ((base >> 3) + t) & (parts - 1)
                for m in range(depth // SUB):
                    at = pl.multiple_of((2 * p + ch) * depth + SUB * m, SUB)
                    block = SUB * (parts * m + t)
                    stage[index, pl.ds(at, SUB)] = g[block : block + SUB]

    def pair(n, _):
        first = 2 * n
        second = jnp.minimum(first + 1, count - 1)

        @pl.when(first + 2 < count)
        def _():
            for copy in loads(first + 2):
                copy.start()

        for copy in loads(first):
            copy.wait()
        slot = 2 * lax.rem(n, 2)
        work = [(first, slot), (second, slot + 1)]
        states = [prepare(p, at) for p, at in work]
        waves = [state[3:] for state in states]
        tabs = [[tab_ref[4 * stage + n] for n in range(4)] for stage in range(4)]
        waves = [forward(right, 1, *wave, tabs[0]) for wave in waves]
        waves = [forward(left, 0, *wave, tabs[1]) for wave in waves]
        waves = [constrain(p, *wave) for (p, _), wave in zip(work, waves)]
        waves = [inverse(left, 0, *wave, tabs[2]) for wave in waves]
        waves = [inverse(right, 1, *wave, tabs[3]) for wave in waves]
        for (p, _), state, wave in zip(work, states, waves):
            put(p, *state[:3], *wave)
        store(n).start()
        return 0

    pairs = (count + 1) >> 1
    lax.fori_loop(0, pairs, pair, 0)

    def stored(p, _):
        store(p).wait()
        return 0

    last.wait()
    lax.fori_loop(0, pairs, stored, 0)


def ordered_kernel(order_ref, turned_ref, amp_ref, out_ref):
    order, turned = order_ref[...], turned_ref[...]
    for p in range(amp_ref.shape[0]):
        rows = dot(order, amp_ref[p]).astype(jnp.bfloat16)
        out_ref[p] = dot(rows, turned).astype(jnp.bfloat16)


def ordered(amplitudes):
    size = amplitudes.shape[1]
    order = np.zeros((size, size), np.float32)
    order[np.arange(size), np.concatenate([np.arange(0, size, 2), np.arange(1, size, 2)])] = 1.0
    vmem = pl.BlockSpec(memory_space=pltpu.VMEM)
    return pl.pallas_call(
        ordered_kernel,
        out_shape=jax.ShapeDtypeStruct(amplitudes.shape, amplitudes.dtype),
        in_specs=[vmem] * 3,
        out_specs=vmem,
        compiler_params=pltpu.CompilerParams(vmem_limit_bytes=16 * MIB),
        cost_estimate=pl.CostEstimate(flops=2**28, bytes_accessed=2 * MIB, transcendentals=0),
        name="ordered",
    )(jnp.asarray(order, jnp.bfloat16), jnp.asarray(order.T, jnp.bfloat16), amplitudes)


def patterns(notes, own, shares, probe, amplitudes):
    rows, size = own.shape[1:]
    slots, parts = amplitudes.shape[0], 2 * len(STEPS)
    depth = size // parts
    length = slots * 2 * depth + SUB
    smem = pl.BlockSpec(memory_space=pltpu.SMEM)
    anywhere = pl.BlockSpec(memory_space=pl.ANY)
    hbm = pl.BlockSpec(memory_space=pltpu.HBM)
    tab = jnp.asarray(tables(size))
    return pl.pallas_call(
        functools.partial(patterns_kernel, size, rows, parts, slots),
        out_shape=jax.ShapeDtypeStruct((parts, length, size), jnp.float32),
        in_specs=[smem] + [hbm] * 4 + [anywhere] * 4,
        out_specs=anywhere,
        scratch_shapes=[
            pltpu.VMEM((4, 2, size + SUB, size), jnp.float32),
            pltpu.VMEM((2, rows // (SUB * parts), parts, SUB, size), jnp.float32),
            pltpu.VMEM(probe.shape, jnp.float32),
            pltpu.VMEM(amplitudes.shape, amplitudes.dtype),
            pltpu.VMEM(tab.shape, tab.dtype),
            pltpu.VMEM((parts, length, size), jnp.float32),
            pltpu.SemaphoreType.DMA((4,)),
            pltpu.SemaphoreType.DMA((3,)),
            pltpu.SemaphoreType.DMA((parts,)),
            pltpu.SemaphoreType.DMA((slots + 1,)),
        ],
        compiler_params=pltpu.CompilerParams(vmem_limit_bytes=40 * MIB),
        cost_estimate=pl.CostEstimate(flops=24 * 2 * size**3 * slots, bytes_accessed=12 * MIB, transcendentals=0),
        name="patterns",
    )(notes, own, probe, amplitudes, tab, *shares)


def place(row, group, parts):
    block = row >> 3
    first = (group - block) & (parts - 1)
    local = (block + first - group) >> (parts.bit_length() - 1)
    return first, pl.multiple_of(local * SUB, SUB), jnp.where(first == 0, row & (SUB - 1), 0)


def each_live(notes_ref, slots, step):
    def device(d, _):
        def pattern(p, _):
            step(d, p, notes_ref[d, p], notes_ref[d, slots + p])
            return 0

        return lax.fori_loop(0, notes_ref[d, 2 * slots], pattern, 0)

    lax.fori_loop(0, notes_ref.shape[0], device, 0)


def gather_kernel(size, parts, slots, group_ref, notes_ref, got_ref, here_ref, next_ref, total):
    depth = size // parts
    group = group_ref[0]
    total[...] = jnp.zeros_like(total)
    column = lax.broadcasted_iota(jnp.int32, (depth, size), 1)
    head_row = lax.broadcasted_iota(jnp.int32, (SUB, size), 0)

    def step(d, p, row, col):
        _, at, shift = place(row, group, parts)
        mine = column >= col
        for ch in range(2):
            block = got_ref[d, pl.ds(pl.multiple_of((2 * p + ch) * depth, depth), depth)]
            for side in range(2):
                part = jnp.where(mine if side == 0 else jnp.logical_not(mine), block, 0.0)
                head = part[:SUB]
                total[side, ch, pl.ds(at, SUB)] += jnp.where(head_row >= shift, head, 0.0)
                total[side, ch, pl.ds(at + SUB, depth - SUB)] += part[SUB:]
                total[side, ch, pl.ds(at + depth, SUB)] += jnp.where(head_row < shift, head, 0.0)

    each_live(notes_ref, slots, step)
    kept = here_ref.shape[1]
    here_ref[...] = total[0, :, :kept]
    next_ref[...] = total[1, :, :kept]


def gathered(group, notes, got, slots, kept):
    parts, length, size = got.shape
    smem = pl.BlockSpec(memory_space=pltpu.SMEM)
    vmem = pl.BlockSpec(memory_space=pltpu.VMEM)
    shape = jax.ShapeDtypeStruct((2, kept, size), jnp.float32)
    return pl.pallas_call(
        functools.partial(gather_kernel, size, parts, slots),
        out_shape=(shape, shape),
        in_specs=[smem, smem, vmem],
        out_specs=(vmem, vmem),
        scratch_shapes=[pltpu.VMEM((2, 2, kept + SUB, size), jnp.float32)],
        compiler_params=pltpu.CompilerParams(vmem_limit_bytes=24 * MIB),
        cost_estimate=pl.CostEstimate(flops=2**22, bytes_accessed=6 * MIB, transcendentals=0),
        name="gathered",
    )(group, notes, got)


def illumination_kernel(size, parts, slots, group_ref, here_ref, before_ref, probe_ref, out_ref, intensity, total):
    depth = size // parts
    group = group_ref[0]
    square = probe_ref[0] * probe_ref[0] + probe_ref[1] * probe_ref[1]
    intensity[:SUB] = square[size - SUB :]
    intensity[SUB:] = square
    total[...] = jnp.zeros_like(total)
    column = lax.broadcasted_iota(jnp.int32, (depth, size), 1)
    head_row = lax.broadcasted_iota(jnp.int32, (SUB, size), 0)

    for side, ref in enumerate((here_ref, before_ref)):

        def step(d, p, row, col):
            first, at, shift = place(row, group, parts)
            down = row & (SUB - 1)
            blocks = []
            for m in range(depth // SUB):
                start = pl.multiple_of((parts * m + first) * SUB, SUB)
                above, below = [pltpu.roll(intensity[pl.ds(start + n * SUB, SUB)], down, 0) for n in range(2)]
                blocks.append(jnp.where(head_row >= down, below, above))
            placed = pltpu.roll(jnp.concatenate(blocks, axis=0), col, 1)
            part = jnp.where(column >= col if side == 0 else column < col, placed, 0.0)
            head = part[:SUB]
            total[pl.ds(at, SUB)] += jnp.where(head_row >= shift, head, 0.0)
            total[pl.ds(at + SUB, depth - SUB)] += part[SUB:]
            total[pl.ds(at + depth, SUB)] += jnp.where(head_row < shift, head, 0.0)

        each_live(ref, slots, step)
    out_ref[...] = total[: out_ref.shape[0]] + REG


def illumination(group, here, before, probe, slots, kept):
    size = probe.shape[1]
    parts = here.shape[0]
    smem = pl.BlockSpec(memory_space=pltpu.SMEM)
    vmem = pl.BlockSpec(memory_space=pltpu.VMEM)
    return pl.pallas_call(
        functools.partial(illumination_kernel, size, parts, slots),
        out_shape=jax.ShapeDtypeStruct((kept, size), jnp.float32),
        in_specs=[smem, smem, smem, vmem],
        out_specs=vmem,
        scratch_shapes=[
            pltpu.VMEM((size + SUB, size), jnp.float32),
            pltpu.VMEM((kept + SUB, size), jnp.float32),
        ],
        compiler_params=pltpu.CompilerParams(vmem_limit_bytes=16 * MIB),
        cost_estimate=pl.CostEstimate(flops=2**22, bytes_accessed=8 * MIB, transcendentals=0),
        name="illumination",
    )(group, here, before, probe)


def assemble_kernel(other, parts, group_ref, ref, *refs):
    out_ref, sems = refs[-2:]
    core = (group_ref[0] & 1) ^ other
    copies = [pltpu.make_async_copy(ref.at[n], out_ref.at[:, :, 2 * n + core], sems.at[n]) for n in range(parts // 2)]
    for copy in copies:
        copy.start()
    for copy in copies:
        copy.wait()


def assembled(group, other, shares, shape, begun=()):
    parts = shape[2]
    anywhere = pl.BlockSpec(memory_space=pl.ANY)
    hbm = pl.BlockSpec(memory_space=pltpu.HBM)
    return pl.pallas_call(
        functools.partial(assemble_kernel, other, parts),
        out_shape=jax.ShapeDtypeStruct(shape, jnp.float32),
        in_specs=[pl.BlockSpec(memory_space=pltpu.SMEM), anywhere] + [hbm] * len(begun),
        out_specs=hbm,
        scratch_shapes=[pltpu.SemaphoreType.DMA((parts // 2,))],
        input_output_aliases={2: 0} if begun else {},
        compiler_params=pltpu.CompilerParams(vmem_limit_bytes=MIB),
        cost_estimate=pl.CostEstimate(flops=0, bytes_accessed=4 * MIB, transcendentals=0),
        name="assembled",
    )(group, shares, *begun)


def passed_along(x, axis, by):
    devices = lax.axis_size(axis)
    pairs = [(i, i + by) for i in range(devices) if 0 <= i + by < devices]
    return lax.ppermute(x, axis, pairs)


def to_chip(x, by):
    devices = lax.axis_size("group")
    return lax.ppermute(x, "group", [(i, (i + 2 * by) % devices) for i in range(devices)])


def to_core(x):
    return lax.ppermute(x, "group", [(i, i ^ 1) for i in range(lax.axis_size("group"))])


def body(object_field, probe, amplitudes, row_offset, col_offset, counts):
    parts = lax.axis_size("group")
    index = lax.axis_index("group")
    group = index[None]
    rows, size = object_field.shape[1:]
    slots = amplitudes.shape[0]
    kept = rows // parts
    blocks = object_field.reshape(2, kept // SUB, parts, SUB, size)

    def share(which):
        return lax.dynamic_index_in_dim(blocks, which, 2, keepdims=False)

    mine = share(index)
    own_notes = jnp.concatenate([row_offset, col_offset, counts])
    far = passed_along(jnp.stack([share((index + 4) % parts), share((index + 2) % parts)]), "tile", -1)
    near, notes_before = lax.optimization_barrier((passed_along(mine, "tile", -1), passed_along(own_notes, "tile", 1)))
    near = jnp.stack([near, to_chip(near, 1)])
    notes = jnp.stack([own_notes, notes_before, jnp.full_like(own_notes, index)])
    sent = patterns(notes, object_field, (near, far, to_core(near), to_core(far)), probe, ordered(amplitudes))
    got = lax.all_to_all(sent, "group", 0, 0)
    notes = got[:, slots * 2 * (size // parts) :, : 2 * slots + 1].astype(jnp.int32)
    notes_here, notes_before = notes[:, 0], notes[:, 1]
    here, spill = gathered(group, notes_here, got, slots, kept)
    spill = passed_along(spill, "tile", 1)
    weight = illumination(group, notes_here, notes_before, probe, slots, kept)
    result = mine + ((here + spill) / weight).reshape(mine.shape)
    chips = parts // 2
    same_core = [list(range(core, parts, 2)) for core in range(2)]
    spread = jnp.broadcast_to(result, (chips, *result.shape))
    shares = lax.all_to_all(spread, "group", 0, 0, axis_index_groups=same_core)
    field = assembled(group, 0, shares, blocks.shape)
    field = assembled(group, 1, to_core(shares), blocks.shape, (field,))
    return field.reshape(object_field.shape)


def solution(mesh):
    in_specs = (
        P(None, None, "tile"),
        P(),
        P(("tile", "group"), None, None),
        P(("tile", "group")),
        P(("tile", "group")),
        P(("tile", "group")),
    )
    out_specs = P(None, None, "tile")
    return jax.shard_map(body, mesh=mesh, in_specs=in_specs, out_specs=out_specs, check_vma=False)
```

```python
import functools
import math

import jax
import jax.numpy as jnp
import numpy as np
from jax import lax
from jax.experimental import pallas as pl
from jax.experimental.pallas import tpu as pltpu
from jax.sharding import PartitionSpec as P

FLOOR = 0.25
REG = 0.5
SUB = 8
MIB = 2**20

STEPS = (0, -2, 4, 2)


def tables(length):
    half = length // 2
    place, freq = np.arange(half)[:, None], np.arange(half)[None, :]
    scale = 1.0 / math.sqrt(length)
    even, odd = [], []
    for parity, out in ((0, even), (1, odd)):
        angle = (place * (2 * freq + parity) % length) * (2.0 * math.pi / length)
        cos, sin = np.cos(angle) * scale, np.sin(angle) * scale
        by_place = np.block([[cos, -sin], [sin, cos]])
        out += [by_place, by_place.T, by_place, by_place.T]
    parts = []
    for table in [table for pair in zip(even, odd) for table in pair]:
        table = table.astype(np.float32)
        high = table.astype(jnp.bfloat16)
        parts += [high, (table - high.astype(np.float32)).astype(jnp.bfloat16)]
    return np.stack(parts)


def split(x):
    high = x.astype(jnp.bfloat16)
    return high, (x - high.astype(jnp.float32)).astype(jnp.bfloat16)


def dot(a, b):
    return jnp.dot(a, b, preferred_element_type=jnp.float32)


def right(x, high_tab, low_tab):
    high, low = split(x)
    return dot(high, high_tab) + dot(low, high_tab) + dot(high, low_tab)


def left(x, high_tab, low_tab):
    high, low = split(x)
    return dot(high_tab, high) + dot(high_tab, low) + dot(low_tab, high)


def halves(x, axis):
    half = x.shape[axis] // 2
    return lax.slice_in_dim(x, 0, half, axis=axis), lax.slice_in_dim(x, half, 2 * half, axis=axis)


def join(parts, axis):
    return jnp.concatenate(parts, axis=axis)


def forward(mul, axis, a, b, tabs):
    (a0, a1), (b0, b1) = halves(a, axis), halves(b, axis)
    even = mul(join([a0 + a1, b0 + b1], axis), tabs[0], tabs[1])
    odd = mul(join([a0 - a1, b0 - b1], axis), tabs[2], tabs[3])
    (a0, b0), (a1, b1) = halves(even, axis), halves(odd, axis)
    return join([a0, a1], axis), join([b0, b1], axis)


def inverse(mul, axis, a, b, tabs):
    (a0, a1), (b0, b1) = halves(a, axis), halves(b, axis)
    even = mul(join([a0, b0], axis), tabs[0], tabs[1])
    odd = mul(join([a1, b1], axis), tabs[2], tabs[3])
    (a0, b0), (a1, b1) = halves(even, axis), halves(odd, axis)
    return join([a0 + a1, a0 - a1], axis), join([b0 + b1, b0 - b1], axis)


def class_of(group, step, other, parts):
    index = (group + step) & (parts - 1)
    return index ^ 1 if other else index


def patterns_kernel(size, rows, parts, slots, notes_ref, own_ref, probe_hbm, amp_hbm, tab_hbm, near_ref, far_ref, other_near_ref, other_far_ref, re_ref, im_ref,
                    own_buf, rim_buf, probe_ref, amp_ref, tab_ref, stage, own_sems, fixed_sems, piece_sems, store_sems):
    count, group = notes_ref[0, 2 * slots], notes_ref[2, 0]
    span = size + SUB
    depth = size // parts

    def start_of(p):
        return pl.multiple_of(notes_ref[0, p] & -SUB, SUB)

    def first_of(p):
        return pl.multiple_of(jnp.minimum(start_of(p), rows - span), SUB)

    def loads(p):
        slot = 2 * lax.rem(p >> 1, 2)
        return [
            pltpu.make_async_copy(
                own_ref.at[:, pl.ds(first_of(jnp.minimum(p + n, count - 1)), span)], own_buf.at[slot + n], own_sems.at[slot + n])
            for n in range(2)
        ]

    def stores(n):
        where = pl.ds(pl.multiple_of(n * 2 * depth, 2 * depth), 2 * depth)
        return [
            pltpu.make_async_copy(stage.at[ch, :, where], ref.at[:, where], store_sems.at[ch, n])
            for ch, ref in enumerate((re_ref, im_ref))
        ]

    fixed = [
        pltpu.make_async_copy(a, b, fixed_sems.at[n])
        for n, (a, b) in enumerate(((probe_hbm, probe_ref), (tab_hbm, tab_ref), (amp_hbm, amp_ref)))
    ]
    rims = []
    for other, refs in enumerate(((near_ref, far_ref), (other_near_ref, other_far_ref))):
        for n, step in enumerate(STEPS):
            index = class_of(group, step, other, parts)
            rims.append(pltpu.make_async_copy(refs[n // 2].at[n % 2], rim_buf.at[:, :, index], piece_sems.at[len(rims)]))
    for copy in loads(0) + rims + fixed:
        copy.start()

    lane = lax.broadcasted_iota(jnp.int32, (SUB, size), 1)
    head_row = lax.broadcasted_iota(jnp.int32, (SUB, size), 0)
    column = lax.broadcasted_iota(jnp.int32, (size, size), 1)
    note = jnp.zeros((SUB, size), jnp.int32)
    for side in range(2):
        for n in range(2 * slots + 1):
            note = jnp.where(jnp.logical_and(head_row == side, lane == n), notes_ref[side, n], note)
    note = note.astype(jnp.float32)
    for part in range(parts):
        stage[0, part, slots * depth :] = note
    notes = pl.ds(slots * depth, SUB)
    last = pltpu.make_async_copy(stage.at[0, :, notes], re_ref.at[:, notes], store_sems.at[0, slots])
    last.start()
    for copy in fixed + rims:
        copy.wait()
    rim = rim_buf.reshape(2, rows, size)

    def moved_down(ref, shift):
        blocks = [pltpu.roll(ref[SUB * n : SUB * (n + 1)], shift, 0) for n in range(size // SUB)]
        return jnp.concatenate([jnp.where(head_row >= shift, here, above) for here, above in zip(blocks, blocks[-1:] + blocks)], axis=0)

    def prepare(p, slot):
        row, col = notes_ref[0, p], notes_ref[0, slots + p]
        base = start_of(p)
        shift = row - base
        pr, pi = [pltpu.roll(moved_down(probe_ref.at[ch], shift), col, 1) for ch in range(2)]
        mine = column >= col
        lead = pl.multiple_of(base - first_of(p), SUB)
        tail = pl.multiple_of(jnp.minimum(lead + size, size), SUB)
        tail_rim = pl.multiple_of(jnp.minimum(base + size, rows - SUB), SUB)

        def window(ch):
            full = jnp.where(mine, own_buf[slot, ch, pl.ds(lead, size)], rim[ch, pl.ds(base, size)])
            wrap = jnp.where(mine[:SUB], own_buf[slot, ch, pl.ds(tail, SUB)], rim[ch, pl.ds(tail_rim, SUB)])
            head = jnp.where(head_row >= shift, full[:SUB], wrap)
            return jnp.concatenate([head, full[SUB:]], axis=0)

        o_re, o_im = window(0), window(1)
        return base, pr, pi, pr * o_re - pi * o_im, pr * o_im + pi * o_re

    def constrain(p, a, b):
        factor = amp_ref[p].astype(jnp.float32) * lax.rsqrt(jnp.maximum(a * a + b * b, FLOOR * FLOOR)) - 1.0
        return a * factor, b * factor

    def put(p, base, pr, pi, a, b):
        for ch, g in enumerate((pr * a + pi * b, pr * b - pi * a)):
            for t in range(parts):
                index = ((base >> 3) + t) & (parts - 1)
                for m in range(depth // SUB):
                    at = pl.multiple_of(p * depth + SUB * m, SUB)
                    block = SUB * (parts * m + t)
                    stage[ch, index, pl.ds(at, SUB)] = g[block : block + SUB]

    def pair(n, _):
        first = 2 * n
        second = jnp.minimum(first + 1, count - 1)

        @pl.when(first + 2 < count)
        def _():
            for copy in loads(first + 2):
                copy.start()

        for copy in loads(first):
            copy.wait()
        slot = 2 * lax.rem(n, 2)
        work = [(first, slot), (second, slot + 1)]
        states = [prepare(p, at) for p, at in work]
        waves = [state[3:] for state in states]
        tabs = [[tab_ref[4 * stage + n] for n in range(4)] for stage in range(4)]
        waves = [forward(right, 1, *wave, tabs[0]) for wave in waves]
        waves = [forward(left, 0, *wave, tabs[1]) for wave in waves]
        waves = [constrain(p, *wave) for (p, _), wave in zip(work, waves)]
        waves = [inverse(left, 0, *wave, tabs[2]) for wave in waves]
        waves = [inverse(right, 1, *wave, tabs[3]) for wave in waves]
        for (p, _), state, wave in zip(work, states, waves):
            put(p, *state[:3], *wave)
        for copy in stores(n):
            copy.start()
        return 0

    pairs = (count + 1) >> 1
    lax.fori_loop(0, pairs, pair, 0)

    def stored(n, _):
        for copy in stores(n):
            copy.wait()
        return 0

    last.wait()
    lax.fori_loop(0, pairs, stored, 0)


def ordered_kernel(order_ref, turned_ref, amp_ref, out_ref):
    order, turned = order_ref[...], turned_ref[...]
    for p in range(amp_ref.shape[0]):
        rows = dot(order, amp_ref[p]).astype(jnp.bfloat16)
        out_ref[p] = dot(rows, turned).astype(jnp.bfloat16)


def ordered(amplitudes):
    size = amplitudes.shape[1]
    order = np.zeros((size, size), np.float32)
    order[np.arange(size), np.concatenate([np.arange(0, size, 2), np.arange(1, size, 2)])] = 1.0
    vmem = pl.BlockSpec(memory_space=pltpu.VMEM)
    return pl.pallas_call(
        ordered_kernel,
        out_shape=jax.ShapeDtypeStruct(amplitudes.shape, amplitudes.dtype),
        in_specs=[vmem] * 3,
        out_specs=vmem,
        compiler_params=pltpu.CompilerParams(vmem_limit_bytes=16 * MIB),
        cost_estimate=pl.CostEstimate(flops=2**28, bytes_accessed=2 * MIB, transcendentals=0),
        name="ordered",
    )(jnp.asarray(order, jnp.bfloat16), jnp.asarray(order.T, jnp.bfloat16), amplitudes)


def patterns(notes, own, shares, probe, amplitudes):
    rows, size = own.shape[1:]
    slots, parts = amplitudes.shape[0], 2 * len(STEPS)
    depth = size // parts
    length = slots * depth
    smem = pl.BlockSpec(memory_space=pltpu.SMEM)
    anywhere = pl.BlockSpec(memory_space=pl.ANY)
    hbm = pl.BlockSpec(memory_space=pltpu.HBM)
    tab = jnp.asarray(tables(size))
    return pl.pallas_call(
        functools.partial(patterns_kernel, size, rows, parts, slots),
        out_shape=[jax.ShapeDtypeStruct((parts, length + extra, size), jnp.float32) for extra in (SUB, 0)],
        in_specs=[smem] + [hbm] * 4 + [anywhere] * 4,
        out_specs=[anywhere] * 2,
        scratch_shapes=[
            pltpu.VMEM((4, 2, size + SUB, size), jnp.float32),
            pltpu.VMEM((2, rows // (SUB * parts), parts, SUB, size), jnp.float32),
            pltpu.VMEM(probe.shape, jnp.float32),
            pltpu.VMEM(amplitudes.shape, amplitudes.dtype),
            pltpu.VMEM(tab.shape, tab.dtype),
            pltpu.VMEM((2, parts, length + SUB, size), jnp.float32),
            pltpu.SemaphoreType.DMA((4,)),
            pltpu.SemaphoreType.DMA((3,)),
            pltpu.SemaphoreType.DMA((parts,)),
            pltpu.SemaphoreType.DMA((2, slots + 1)),
        ],
        compiler_params=pltpu.CompilerParams(vmem_limit_bytes=40 * MIB),
        cost_estimate=pl.CostEstimate(flops=24 * 2 * size**3 * slots, bytes_accessed=12 * MIB, transcendentals=0),
        name="patterns",
    )(notes, own, probe, amplitudes, tab, *shares)


def place(row, group, parts):
    block = row >> 3
    first = (group - block) & (parts - 1)
    local = (block + first - group) >> (parts.bit_length() - 1)
    return first, pl.multiple_of(local * SUB, SUB), jnp.where(first == 0, row & (SUB - 1), 0)


def each_live(notes_ref, slots, step):
    def device(d, _):
        def pattern(p, _):
            step(d, p, notes_ref[d, p], notes_ref[d, slots + p])
            return 0

        return lax.fori_loop(0, notes_ref[d, 2 * slots], pattern, 0)

    lax.fori_loop(0, notes_ref.shape[0], device, 0)


def gather_kernel(size, parts, slots, group_ref, notes_ref, got_ref, here_ref, next_ref, total):
    depth = size // parts
    group = group_ref[0]
    total[...] = jnp.zeros_like(total)
    column = lax.broadcasted_iota(jnp.int32, (depth, size), 1)
    head_row = lax.broadcasted_iota(jnp.int32, (SUB, size), 0)

    def step(d, p, row, col):
        _, at, shift = place(row, group, parts)
        mine = column >= col
        block = got_ref[d, pl.ds(pl.multiple_of(p * depth, depth), depth)]
        for side in range(2):
            part = jnp.where(mine if side == 0 else jnp.logical_not(mine), block, 0.0)
            head = part[:SUB]
            total[side, pl.ds(at, SUB)] += jnp.where(head_row >= shift, head, 0.0)
            total[side, pl.ds(at + SUB, depth - SUB)] += part[SUB:]
            total[side, pl.ds(at + depth, SUB)] += jnp.where(head_row < shift, head, 0.0)

    each_live(notes_ref, slots, step)
    kept = here_ref.shape[0]
    here_ref[...] = total[0, :kept]
    next_ref[...] = total[1, :kept]


def gathered(group, notes, got, slots, kept):
    parts, _, size = got.shape
    smem = pl.BlockSpec(memory_space=pltpu.SMEM)
    vmem = pl.BlockSpec(memory_space=pltpu.VMEM)
    shape = jax.ShapeDtypeStruct((kept, size), jnp.float32)
    return pl.pallas_call(
        functools.partial(gather_kernel, size, parts, slots),
        out_shape=(shape, shape),
        in_specs=[smem, smem, vmem],
        out_specs=(vmem, vmem),
        scratch_shapes=[pltpu.VMEM((2, kept + SUB, size), jnp.float32)],
        compiler_params=pltpu.CompilerParams(vmem_limit_bytes=8 * MIB),
        cost_estimate=pl.CostEstimate(flops=2**21, bytes_accessed=3 * MIB, transcendentals=0),
        name="gathered",
    )(group, notes, got)


def illumination_kernel(size, parts, slots, group_ref, here_ref, before_ref, probe_ref, out_ref, intensity, total):
    depth = size // parts
    group = group_ref[0]
    square = probe_ref[0] * probe_ref[0] + probe_ref[1] * probe_ref[1]
    intensity[:SUB] = square[size - SUB :]
    intensity[SUB:] = square
    total[...] = jnp.zeros_like(total)
    column = lax.broadcasted_iota(jnp.int32, (depth, size), 1)
    head_row = lax.broadcasted_iota(jnp.int32, (SUB, size), 0)

    for side, ref in enumerate((here_ref, before_ref)):

        def step(d, p, row, col):
            first, at, shift = place(row, group, parts)
            down = row & (SUB - 1)
            blocks = []
            for m in range(depth // SUB):
                start = pl.multiple_of((parts * m + first) * SUB, SUB)
                above, below = [pltpu.roll(intensity[pl.ds(start + n * SUB, SUB)], down, 0) for n in range(2)]
                blocks.append(jnp.where(head_row >= down, below, above))
            placed = pltpu.roll(jnp.concatenate(blocks, axis=0), col, 1)
            part = jnp.where(column >= col if side == 0 else column < col, placed, 0.0)
            head = part[:SUB]
            total[pl.ds(at, SUB)] += jnp.where(head_row >= shift, head, 0.0)
            total[pl.ds(at + SUB, depth - SUB)] += part[SUB:]
            total[pl.ds(at + depth, SUB)] += jnp.where(head_row < shift, head, 0.0)

        each_live(ref, slots, step)
    out_ref[...] = total[: out_ref.shape[0]] + REG


def illumination(group, here, before, probe, slots, kept):
    size = probe.shape[1]
    parts = here.shape[0]
    smem = pl.BlockSpec(memory_space=pltpu.SMEM)
    vmem = pl.BlockSpec(memory_space=pltpu.VMEM)
    return pl.pallas_call(
        functools.partial(illumination_kernel, size, parts, slots),
        out_shape=jax.ShapeDtypeStruct((kept, size), jnp.float32),
        in_specs=[smem, smem, smem, vmem],
        out_specs=vmem,
        scratch_shapes=[
            pltpu.VMEM((size + SUB, size), jnp.float32),
            pltpu.VMEM((kept + SUB, size), jnp.float32),
        ],
        compiler_params=pltpu.CompilerParams(vmem_limit_bytes=4 * MIB),
        cost_estimate=pl.CostEstimate(flops=2**22, bytes_accessed=8 * MIB, transcendentals=0),
        name="illumination",
    )(group, here, before, probe)


def assemble_kernel(kinds, parts, staged, group_ref, *refs):
    sources = list(refs[: len(kinds)])
    if staged:
        out_ref, held, load_sems, sems = refs[-4:]
        loads = [pltpu.make_async_copy(ref, held.at[n], load_sems.at[n]) for n, ref in enumerate(sources)]
        sources = [held.at[n] for n in range(len(kinds))]
    else:
        (out_ref, sems), loads = refs[-2:], []
    for load in loads:
        load.start()
    copies = []
    for k, (ch, other) in enumerate(kinds):
        core = (group_ref[0] & 1) ^ other
        if loads:
            loads[k].wait()
        for n in range(parts // 2):
            copies.append(pltpu.make_async_copy(sources[k].at[n], out_ref.at[ch, :, 2 * n + core], sems.at[len(copies)]))
            copies[-1].start()
    for copy in copies:
        copy.wait()


def assembled(group, kinds, shares, shape, begun=(), staged=True):
    parts = shape[2]
    anywhere = pl.BlockSpec(memory_space=pl.ANY)
    hbm = pl.BlockSpec(memory_space=pltpu.HBM)
    count = len(shares)
    held = [pltpu.VMEM((count, *shares[0].shape), jnp.float32), pltpu.SemaphoreType.DMA((count,))] if staged else []
    return pl.pallas_call(
        functools.partial(assemble_kernel, kinds, parts, staged),
        out_shape=jax.ShapeDtypeStruct(shape, jnp.float32),
        in_specs=[pl.BlockSpec(memory_space=pltpu.SMEM)] + [anywhere] * count + [hbm] * len(begun),
        out_specs=hbm,
        scratch_shapes=held + [pltpu.SemaphoreType.DMA((count * parts // 2,))],
        input_output_aliases={1 + count: 0} if begun else {},
        compiler_params=pltpu.CompilerParams(vmem_limit_bytes=5 * MIB if staged else MIB),
        cost_estimate=pl.CostEstimate(flops=0, bytes_accessed=2 * count * MIB, transcendentals=0),
        name="assembled",
    )(group, *shares, *begun)


def passed_along(x, axis, by):
    devices = lax.axis_size(axis)
    pairs = [(i, i + by) for i in range(devices) if 0 <= i + by < devices]
    return lax.ppermute(x, axis, pairs)


def to_chip(x, by):
    devices = lax.axis_size("group")
    return lax.ppermute(x, "group", [(i, (i + 2 * by) % devices) for i in range(devices)])


def to_core(x):
    return lax.ppermute(x, "group", [(i, i ^ 1) for i in range(lax.axis_size("group"))])


def body(object_field, probe, amplitudes, row_offset, col_offset, counts):
    parts = lax.axis_size("group")
    index = lax.axis_index("group")
    group = index[None]
    rows, size = object_field.shape[1:]
    slots = amplitudes.shape[0]
    kept = rows // parts
    blocks = object_field.reshape(2, kept // SUB, parts, SUB, size)

    def cut(source, which):
        return lax.dynamic_index_in_dim(source, which, 2, keepdims=False)

    own_notes = jnp.concatenate([row_offset, col_offset, counts])
    far = passed_along(jnp.stack([cut(blocks, (index + 4) % parts), cut(blocks, (index + 2) % parts)]), "tile", -1)
    near, notes_before = lax.optimization_barrier((passed_along(cut(blocks, index), "tile", -1), passed_along(own_notes, "tile", 1)))
    near = jnp.stack([near, to_chip(near, 1)])
    notes = jnp.stack([own_notes, notes_before, jnp.full_like(own_notes, index)])
    sent = patterns(notes, object_field, (near, far, to_core(near), to_core(far)), probe, ordered(amplitudes))
    blocks, first = lax.optimization_barrier((blocks, sent[0]))
    sent = (first, sent[1])
    mine = cut(blocks, index)
    gots = [lax.all_to_all(channel, "group", 0, 0) for channel in sent]
    notes = gots[0][:, slots * (size // parts) :, : 2 * slots + 1].astype(jnp.int32)
    notes_here, notes_before = notes[:, 0], notes[:, 1]
    weight = illumination(group, notes_here, notes_before, probe, slots, kept)
    chips = parts // 2
    same_core = [list(range(core, parts, 2)) for core in range(2)]
    spreads = []
    for ch, got in enumerate(gots):
        here, spill = gathered(group, notes_here, got, slots, kept)
        spill = passed_along(spill, "tile", 1)
        if spreads:
            spill, _ = lax.optimization_barrier((spill, spreads[0]))
        result = mine[ch] + ((here + spill) / weight).reshape(mine.shape[1:])
        spreads.append(jnp.broadcast_to(result, (chips, *result.shape)))
    shares = [lax.all_to_all(spread, "group", 0, 0, axis_index_groups=same_core) for spread in spreads]
    others = [to_core(share) for share in shares]
    field = assembled(group, ((0, 0), (1, 0), (0, 1)), (*shares, others[0]), blocks.shape)
    field = assembled(group, ((1, 1),), (others[1],), blocks.shape, (field,), staged=False)
    return field.reshape(object_field.shape)


def solution(mesh):
    in_specs = (
        P(None, None, "tile"),
        P(),
        P(("tile", "group"), None, None),
        P(("tile", "group")),
        P(("tile", "group")),
        P(("tile", "group")),
    )
    out_specs = P(None, None, "tile")
    return jax.shard_map(body, mesh=mesh, in_specs=in_specs, out_specs=out_specs, check_vma=False)
```

```python
import functools
import math

import jax
import jax.numpy as jnp
import numpy as np
from jax import lax
from jax.experimental import pallas as pl
from jax.experimental.pallas import tpu as pltpu
from jax.sharding import PartitionSpec as P

FLOOR = 0.25
REG = 0.5
SUB = 8
MIB = 2**20

STEPS = (0, -2, 4, 2)


def tables(length):
    half = length // 2
    place, freq = np.arange(half)[:, None], np.arange(half)[None, :]
    scale = 1.0 / math.sqrt(length)
    even, odd = [], []
    for parity, out in ((0, even), (1, odd)):
        angle = (place * (2 * freq + parity) % length) * (2.0 * math.pi / length)
        cos, sin = np.cos(angle) * scale, np.sin(angle) * scale
        by_place = np.block([[cos, -sin], [sin, cos]])
        out += [by_place, by_place.T, by_place, by_place.T]
    parts = []
    for table in [table for pair in zip(even, odd) for table in pair]:
        table = table.astype(np.float32)
        high = table.astype(jnp.bfloat16)
        parts += [high, (table - high.astype(np.float32)).astype(jnp.bfloat16)]
    return np.stack(parts)


def split(x):
    high = x.astype(jnp.bfloat16)
    return high, (x - high.astype(jnp.float32)).astype(jnp.bfloat16)


def dot(a, b):
    return jnp.dot(a, b, preferred_element_type=jnp.float32)


def right(x, high_tab, low_tab):
    high, low = split(x)
    return dot(high, high_tab) + dot(low, high_tab) + dot(high, low_tab)


def left(x, high_tab, low_tab):
    high, low = split(x)
    return dot(high_tab, high) + dot(high_tab, low) + dot(low_tab, high)


def halves(x, axis):
    half = x.shape[axis] // 2
    return lax.slice_in_dim(x, 0, half, axis=axis), lax.slice_in_dim(x, half, 2 * half, axis=axis)


def join(parts, axis):
    return jnp.concatenate(parts, axis=axis)


def forward(mul, axis, a, b, tabs):
    (a0, a1), (b0, b1) = halves(a, axis), halves(b, axis)
    even = mul(join([a0 + a1, b0 + b1], axis), tabs[0], tabs[1])
    odd = mul(join([a0 - a1, b0 - b1], axis), tabs[2], tabs[3])
    (a0, b0), (a1, b1) = halves(even, axis), halves(odd, axis)
    return join([a0, a1], axis), join([b0, b1], axis)


def inverse(mul, axis, a, b, tabs):
    (a0, a1), (b0, b1) = halves(a, axis), halves(b, axis)
    even = mul(join([a0, b0], axis), tabs[0], tabs[1])
    odd = mul(join([a1, b1], axis), tabs[2], tabs[3])
    (a0, b0), (a1, b1) = halves(even, axis), halves(odd, axis)
    return join([a0 + a1, a0 - a1], axis), join([b0 + b1, b0 - b1], axis)


def class_of(group, step, other, parts):
    index = (group + step) & (parts - 1)
    return index ^ 1 if other else index


def patterns_kernel(size, rows, parts, slots, notes_ref, own_ref, probe_hbm, amp_hbm, tab_hbm, near_ref, far_ref, other_near_ref, other_far_ref, re_ref, im_ref,
                    own_buf, rim_buf, probe_ref, amp_ref, tab_ref, stage, own_sems, fixed_sems, piece_sems, store_sems):
    count, group = notes_ref[0, 2 * slots], notes_ref[2, 0]
    span = size + SUB
    depth = size // parts

    def start_of(p):
        return pl.multiple_of(notes_ref[0, p] & -SUB, SUB)

    def first_of(p):
        return pl.multiple_of(jnp.minimum(start_of(p), rows - span), SUB)

    def loads(p):
        slot = 2 * lax.rem(p >> 1, 2)
        return [
            pltpu.make_async_copy(
                own_ref.at[:, pl.ds(first_of(jnp.minimum(p + n, count - 1)), span)], own_buf.at[slot + n], own_sems.at[slot + n])
            for n in range(2)
        ]

    def stores(n):
        where = pl.ds(pl.multiple_of(n * 2 * depth, 2 * depth), 2 * depth)
        return [
            pltpu.make_async_copy(stage.at[ch, :, where], ref.at[:, where], store_sems.at[ch, n])
            for ch, ref in enumerate((re_ref, im_ref))
        ]

    fixed = [
        pltpu.make_async_copy(a, b, fixed_sems.at[n])
        for n, (a, b) in enumerate(((probe_hbm, probe_ref), (tab_hbm, tab_ref), (amp_hbm, amp_ref)))
    ]
    rims = []
    for other, refs in enumerate(((near_ref, far_ref), (other_near_ref, other_far_ref))):
        for n, step in enumerate(STEPS):
            index = class_of(group, step, other, parts)
            rims.append(pltpu.make_async_copy(refs[n // 2].at[n % 2], rim_buf.at[:, :, index], piece_sems.at[len(rims)]))
    for copy in loads(0) + rims + fixed:
        copy.start()

    lane = lax.broadcasted_iota(jnp.int32, (SUB, size), 1)
    head_row = lax.broadcasted_iota(jnp.int32, (SUB, size), 0)
    column = lax.broadcasted_iota(jnp.int32, (size, size), 1)
    note = jnp.zeros((SUB, size), jnp.int32)
    for side in range(2):
        for n in range(2 * slots + 1):
            note = jnp.where(jnp.logical_and(head_row == side, lane == n), notes_ref[side, n], note)
    note = note.astype(jnp.float32)
    for part in range(parts):
        stage[0, part, slots * depth :] = note
    notes = pl.ds(slots * depth, SUB)
    last = pltpu.make_async_copy(stage.at[0, :, notes], re_ref.at[:, notes], store_sems.at[0, slots])
    last.start()
    for copy in fixed + rims:
        copy.wait()
    rim = rim_buf.reshape(2, rows, size)

    def moved_down(ref, shift):
        blocks = [pltpu.roll(ref[SUB * n : SUB * (n + 1)], shift, 0) for n in range(size // SUB)]
        return jnp.concatenate([jnp.where(head_row >= shift, here, above) for here, above in zip(blocks, blocks[-1:] + blocks)], axis=0)

    def prepare(p, slot):
        row, col = notes_ref[0, p], notes_ref[0, slots + p]
        base = start_of(p)
        shift = row - base
        pr, pi = [pltpu.roll(moved_down(probe_ref.at[ch], shift), col, 1) for ch in range(2)]
        mine = column >= col
        lead = pl.multiple_of(base - first_of(p), SUB)
        tail = pl.multiple_of(jnp.minimum(lead + size, size), SUB)
        tail_rim = pl.multiple_of(jnp.minimum(base + size, rows - SUB), SUB)

        def window(ch):
            full = jnp.where(mine, own_buf[slot, ch, pl.ds(lead, size)], rim[ch, pl.ds(base, size)])
            wrap = jnp.where(mine[:SUB], own_buf[slot, ch, pl.ds(tail, SUB)], rim[ch, pl.ds(tail_rim, SUB)])
            head = jnp.where(head_row >= shift, full[:SUB], wrap)
            return jnp.concatenate([head, full[SUB:]], axis=0)

        o_re, o_im = window(0), window(1)
        return base, pr, pi, pr * o_re - pi * o_im, pr * o_im + pi * o_re

    def constrain(p, a, b):
        factor = amp_ref[p].astype(jnp.float32) * lax.rsqrt(jnp.maximum(a * a + b * b, FLOOR * FLOOR)) - 1.0
        return a * factor, b * factor

    def put(p, base, pr, pi, a, b):
        for ch, g in enumerate((pr * a + pi * b, pr * b - pi * a)):
            for t in range(parts):
                index = ((base >> 3) + t) & (parts - 1)
                for m in range(depth // SUB):
                    at = pl.multiple_of(p * depth + SUB * m, SUB)
                    block = SUB * (parts * m + t)
                    stage[ch, index, pl.ds(at, SUB)] = g[block : block + SUB]

    def pair(n, _):
        first = 2 * n
        second = jnp.minimum(first + 1, count - 1)

        @pl.when(first + 2 < count)
        def _():
            for copy in loads(first + 2):
                copy.start()

        for copy in loads(first):
            copy.wait()
        slot = 2 * lax.rem(n, 2)
        work = [(first, slot), (second, slot + 1)]
        states = [prepare(p, at) for p, at in work]
        waves = [state[3:] for state in states]
        tabs = [[tab_ref[4 * stage + n] for n in range(4)] for stage in range(4)]
        waves = [forward(right, 1, *wave, tabs[0]) for wave in waves]
        waves = [forward(left, 0, *wave, tabs[1]) for wave in waves]
        waves = [constrain(p, *wave) for (p, _), wave in zip(work, waves)]
        waves = [inverse(left, 0, *wave, tabs[2]) for wave in waves]
        waves = [inverse(right, 1, *wave, tabs[3]) for wave in waves]
        for (p, _), state, wave in zip(work, states, waves):
            put(p, *state[:3], *wave)
        for copy in stores(n):
            copy.start()
        return 0

    pairs = (count + 1) >> 1
    lax.fori_loop(0, pairs, pair, 0)

    def stored(n, _):
        for copy in stores(n):
            copy.wait()
        return 0

    last.wait()
    lax.fori_loop(0, pairs, stored, 0)


def ordered_kernel(order_ref, turned_ref, amp_ref, out_ref):
    order, turned = order_ref[...], turned_ref[...]
    for p in range(amp_ref.shape[0]):
        rows = dot(order, amp_ref[p]).astype(jnp.bfloat16)
        out_ref[p] = dot(rows, turned).astype(jnp.bfloat16)


def ordered(amplitudes):
    size = amplitudes.shape[1]
    order = np.zeros((size, size), np.float32)
    order[np.arange(size), np.concatenate([np.arange(0, size, 2), np.arange(1, size, 2)])] = 1.0
    vmem = pl.BlockSpec(memory_space=pltpu.VMEM)
    return pl.pallas_call(
        ordered_kernel,
        out_shape=jax.ShapeDtypeStruct(amplitudes.shape, amplitudes.dtype),
        in_specs=[vmem] * 3,
        out_specs=vmem,
        compiler_params=pltpu.CompilerParams(vmem_limit_bytes=16 * MIB),
        cost_estimate=pl.CostEstimate(flops=2**28, bytes_accessed=2 * MIB, transcendentals=0),
        name="ordered",
    )(jnp.asarray(order, jnp.bfloat16), jnp.asarray(order.T, jnp.bfloat16), amplitudes)


def patterns(notes, own, shares, probe, amplitudes):
    rows, size = own.shape[1:]
    slots, parts = amplitudes.shape[0], 2 * len(STEPS)
    depth = size // parts
    length = slots * depth
    smem = pl.BlockSpec(memory_space=pltpu.SMEM)
    anywhere = pl.BlockSpec(memory_space=pl.ANY)
    hbm = pl.BlockSpec(memory_space=pltpu.HBM)
    tab = jnp.asarray(tables(size))
    return pl.pallas_call(
        functools.partial(patterns_kernel, size, rows, parts, slots),
        out_shape=[jax.ShapeDtypeStruct((parts, length + extra, size), jnp.float32) for extra in (SUB, 0)],
        in_specs=[smem] + [hbm] * 4 + [anywhere] * 4,
        out_specs=[anywhere] * 2,
        scratch_shapes=[
            pltpu.VMEM((4, 2, size + SUB, size), jnp.float32),
            pltpu.VMEM((2, rows // (SUB * parts), parts, SUB, size), jnp.float32),
            pltpu.VMEM(probe.shape, jnp.float32),
            pltpu.VMEM(amplitudes.shape, amplitudes.dtype),
            pltpu.VMEM(tab.shape, tab.dtype),
            pltpu.VMEM((2, parts, length + SUB, size), jnp.float32),
            pltpu.SemaphoreType.DMA((4,)),
            pltpu.SemaphoreType.DMA((3,)),
            pltpu.SemaphoreType.DMA((parts,)),
            pltpu.SemaphoreType.DMA((2, slots + 1)),
        ],
        compiler_params=pltpu.CompilerParams(vmem_limit_bytes=40 * MIB),
        cost_estimate=pl.CostEstimate(flops=24 * 2 * size**3 * slots, bytes_accessed=12 * MIB, transcendentals=0),
        name="patterns",
    )(notes, own, probe, amplitudes, tab, *shares)


def place(row, group, parts):
    block = row >> 3
    first = (group - block) & (parts - 1)
    local = (block + first - group) >> (parts.bit_length() - 1)
    return first, pl.multiple_of(local * SUB, SUB), jnp.where(first == 0, row & (SUB - 1), 0)


def each_live(notes_ref, slots, step):
    def device(d, _):
        def pattern(p, _):
            step(d, p, notes_ref[d, p], notes_ref[d, slots + p])
            return 0

        return lax.fori_loop(0, notes_ref[d, 2 * slots], pattern, 0)

    lax.fori_loop(0, notes_ref.shape[0], device, 0)


def gather_kernel(size, parts, slots, group_ref, notes_ref, got_ref, here_ref, next_ref, total):
    depth = size // parts
    group = group_ref[0]
    total[...] = jnp.zeros_like(total)
    column = lax.broadcasted_iota(jnp.int32, (depth, size), 1)
    head_row = lax.broadcasted_iota(jnp.int32, (SUB, size), 0)

    def step(d, p, row, col):
        _, at, shift = place(row, group, parts)
        mine = column >= col
        block = got_ref[d, pl.ds(pl.multiple_of(p * depth, depth), depth)]
        for side in range(2):
            part = jnp.where(mine if side == 0 else jnp.logical_not(mine), block, 0.0)
            head = part[:SUB]
            total[side, pl.ds(at, SUB)] += jnp.where(head_row >= shift, head, 0.0)
            total[side, pl.ds(at + SUB, depth - SUB)] += part[SUB:]
            total[side, pl.ds(at + depth, SUB)] += jnp.where(head_row < shift, head, 0.0)

    each_live(notes_ref, slots, step)
    kept = here_ref.shape[0]
    here_ref[...] = total[0, :kept]
    next_ref[...] = total[1, :kept]


def gathered(group, notes, got, slots, kept):
    parts, _, size = got.shape
    smem = pl.BlockSpec(memory_space=pltpu.SMEM)
    vmem = pl.BlockSpec(memory_space=pltpu.VMEM)
    shape = jax.ShapeDtypeStruct((kept, size), jnp.float32)
    return pl.pallas_call(
        functools.partial(gather_kernel, size, parts, slots),
        out_shape=(shape, shape),
        in_specs=[smem, smem, vmem],
        out_specs=(vmem, vmem),
        scratch_shapes=[pltpu.VMEM((2, kept + SUB, size), jnp.float32)],
        compiler_params=pltpu.CompilerParams(vmem_limit_bytes=8 * MIB),
        cost_estimate=pl.CostEstimate(flops=2**21, bytes_accessed=3 * MIB, transcendentals=0),
        name="gathered",
    )(group, notes, got)


def illumination_kernel(size, parts, slots, group_ref, here_ref, before_ref, probe_ref, out_ref, intensity, total):
    depth = size // parts
    group = group_ref[0]
    square = probe_ref[0] * probe_ref[0] + probe_ref[1] * probe_ref[1]
    intensity[:SUB] = square[size - SUB :]
    intensity[SUB:] = square
    total[...] = jnp.zeros_like(total)
    column = lax.broadcasted_iota(jnp.int32, (depth, size), 1)
    head_row = lax.broadcasted_iota(jnp.int32, (SUB, size), 0)

    for side, ref in enumerate((here_ref, before_ref)):

        def step(d, p, row, col):
            first, at, shift = place(row, group, parts)
            down = row & (SUB - 1)
            blocks = []
            for m in range(depth // SUB):
                start = pl.multiple_of((parts * m + first) * SUB, SUB)
                above, below = [pltpu.roll(intensity[pl.ds(start + n * SUB, SUB)], down, 0) for n in range(2)]
                blocks.append(jnp.where(head_row >= down, below, above))
            placed = pltpu.roll(jnp.concatenate(blocks, axis=0), col, 1)
            part = jnp.where(column >= col if side == 0 else column < col, placed, 0.0)
            head = part[:SUB]
            total[pl.ds(at, SUB)] += jnp.where(head_row >= shift, head, 0.0)
            total[pl.ds(at + SUB, depth - SUB)] += part[SUB:]
            total[pl.ds(at + depth, SUB)] += jnp.where(head_row < shift, head, 0.0)

        each_live(ref, slots, step)
    out_ref[...] = total[: out_ref.shape[0]] + REG


def illumination(group, here, before, probe, slots, kept):
    size = probe.shape[1]
    parts = here.shape[0]
    smem = pl.BlockSpec(memory_space=pltpu.SMEM)
    vmem = pl.BlockSpec(memory_space=pltpu.VMEM)
    return pl.pallas_call(
        functools.partial(illumination_kernel, size, parts, slots),
        out_shape=jax.ShapeDtypeStruct((kept, size), jnp.float32),
        in_specs=[smem, smem, smem, vmem],
        out_specs=vmem,
        scratch_shapes=[
            pltpu.VMEM((size + SUB, size), jnp.float32),
            pltpu.VMEM((kept + SUB, size), jnp.float32),
        ],
        compiler_params=pltpu.CompilerParams(vmem_limit_bytes=4 * MIB),
        cost_estimate=pl.CostEstimate(flops=2**22, bytes_accessed=8 * MIB, transcendentals=0),
        name="illumination",
    )(group, here, before, probe)


def assemble_kernel(kinds, parts, staged, group_ref, *refs):
    sources = list(refs[: len(kinds)])
    if staged:
        out_ref, held, load_sems, sems = refs[-4:]
        loads = [pltpu.make_async_copy(ref, held.at[n], load_sems.at[n]) for n, ref in enumerate(sources)]
        sources = [held.at[n] for n in range(len(kinds))]
    else:
        (out_ref, sems), loads = refs[-2:], []
    for load in loads:
        load.start()
    copies = []
    for k, (ch, other) in enumerate(kinds):
        core = (group_ref[0] & 1) ^ other
        if loads:
            loads[k].wait()
        for n in range(parts // 2):
            copies.append(pltpu.make_async_copy(sources[k].at[n], out_ref.at[ch, :, 2 * n + core], sems.at[len(copies)]))
            copies[-1].start()
    for copy in copies:
        copy.wait()


def assembled(group, kinds, shares, shape, begun=(), staged=True):
    parts = shape[2]
    anywhere = pl.BlockSpec(memory_space=pl.ANY)
    hbm = pl.BlockSpec(memory_space=pltpu.HBM)
    count = len(shares)
    held = [pltpu.VMEM((count, *shares[0].shape), jnp.float32), pltpu.SemaphoreType.DMA((count,))] if staged else []
    return pl.pallas_call(
        functools.partial(assemble_kernel, kinds, parts, staged),
        out_shape=jax.ShapeDtypeStruct(shape, jnp.float32),
        in_specs=[pl.BlockSpec(memory_space=pltpu.SMEM)] + [anywhere] * count + [hbm] * len(begun),
        out_specs=hbm,
        scratch_shapes=held + [pltpu.SemaphoreType.DMA((count * parts // 2,))],
        input_output_aliases={1 + count: 0} if begun else {},
        compiler_params=pltpu.CompilerParams(vmem_limit_bytes=5 * MIB if staged else MIB),
        cost_estimate=pl.CostEstimate(flops=0, bytes_accessed=2 * count * MIB, transcendentals=0),
        name="assembled",
    )(group, *shares, *begun)


def passed_along(x, axis, by):
    devices = lax.axis_size(axis)
    pairs = [(i, i + by) for i in range(devices) if 0 <= i + by < devices]
    return lax.ppermute(x, axis, pairs)


def to_chip(x, by):
    devices = lax.axis_size("group")
    return lax.ppermute(x, "group", [(i, (i + 2 * by) % devices) for i in range(devices)])


def to_core(x):
    return lax.ppermute(x, "group", [(i, i ^ 1) for i in range(lax.axis_size("group"))])


def body(object_field, probe, amplitudes, row_offset, col_offset, counts):
    parts = lax.axis_size("group")
    index = lax.axis_index("group")
    group = index[None]
    rows, size = object_field.shape[1:]
    slots = amplitudes.shape[0]
    kept = rows // parts
    blocks = object_field.reshape(2, kept // SUB, parts, SUB, size)

    def cut(source, which):
        return lax.dynamic_index_in_dim(source, which, 2, keepdims=False)

    own_notes = jnp.concatenate([row_offset, col_offset, counts])
    far = passed_along(jnp.stack([cut(blocks, (index + 4) % parts), cut(blocks, (index + 2) % parts)]), "tile", -1)
    near, notes_before = lax.optimization_barrier((passed_along(cut(blocks, index), "tile", -1), passed_along(own_notes, "tile", 1)))
    near = jnp.stack([near, to_chip(near, 1)])
    notes = jnp.stack([own_notes, notes_before, jnp.full_like(own_notes, index)])
    sent = patterns(notes, object_field, (near, far, to_core(near), to_core(far)), probe, ordered(amplitudes))
    blocks, first = lax.optimization_barrier((blocks, sent[0]))
    sent = (first, sent[1])
    mine = cut(blocks, index)
    gots = [lax.all_to_all(channel, "group", 0, 0) for channel in sent]
    notes = gots[0][:, slots * (size // parts) :, : 2 * slots + 1].astype(jnp.int32)
    notes_here, notes_before = notes[:, 0], notes[:, 1]
    weight = illumination(group, notes_here, notes_before, probe, slots, kept)
    chips = parts // 2
    same_core = [list(range(core, parts, 2)) for core in range(2)]
    spreads = []
    for ch, got in enumerate(gots):
        here, spill = gathered(group, notes_here, got, slots, kept)
        spill = passed_along(spill, "tile", 1)
        if spreads:
            spill, _ = lax.optimization_barrier((spill, spreads[0]))
        result = mine[ch] + ((here + spill) / weight).reshape(mine.shape[1:])
        spreads.append(jnp.broadcast_to(result, (chips, *result.shape)))
    shares = [lax.all_to_all(spreads[0], "group", 0, 0, axis_index_groups=same_core)]
    shares[0], spreads[1] = lax.optimization_barrier((shares[0], spreads[1]))
    shares.append(lax.all_to_all(spreads[1], "group", 0, 0, axis_index_groups=same_core))
    field = assembled(group, ((0, 0),), shares[:1], blocks.shape)
    shares[1], field = lax.optimization_barrier((shares[1], field))
    others = [to_core(share) for share in shares]
    field = assembled(group, ((1, 0), (0, 1)), (shares[1], others[0]), blocks.shape, (field,))
    field = assembled(group, ((1, 1),), (others[1],), blocks.shape, (field,), staged=False)
    return field.reshape(object_field.shape)


def solution(mesh):
    in_specs = (
        P(None, None, "tile"),
        P(),
        P(("tile", "group"), None, None),
        P(("tile", "group")),
        P(("tile", "group")),
        P(("tile", "group")),
    )
    out_specs = P(None, None, "tile")
    return jax.shard_map(body, mesh=mesh, in_specs=in_specs, out_specs=out_specs, check_vma=False)
```

```python
import functools
import math

import jax
import jax.numpy as jnp
import numpy as np
from jax import lax
from jax.experimental import pallas as pl
from jax.experimental.pallas import tpu as pltpu
from jax.sharding import PartitionSpec as P

FLOOR = 0.25
REG = 0.5
SUB = 8
MIB = 2**20

STEPS = (0, -2, 4, 2)


def tables(length):
    half = length // 2
    place, freq = np.arange(half)[:, None], np.arange(half)[None, :]
    scale = 1.0 / math.sqrt(length)
    even, odd = [], []
    for parity, out in ((0, even), (1, odd)):
        angle = (place * (2 * freq + parity) % length) * (2.0 * math.pi / length)
        cos, sin = np.cos(angle) * scale, np.sin(angle) * scale
        by_place = np.block([[cos, -sin], [sin, cos]])
        out += [by_place, by_place.T, by_place, by_place.T]
    parts = []
    for table in [table for pair in zip(even, odd) for table in pair]:
        table = table.astype(np.float32)
        high = table.astype(jnp.bfloat16)
        parts += [high, (table - high.astype(np.float32)).astype(jnp.bfloat16)]
    return np.stack(parts)


def split(x):
    high = x.astype(jnp.bfloat16)
    return high, (x - high.astype(jnp.float32)).astype(jnp.bfloat16)


def dot(a, b):
    return jnp.dot(a, b, preferred_element_type=jnp.float32)


def right(x, high_tab, low_tab):
    high, low = split(x)
    return dot(high, high_tab) + dot(low, high_tab) + dot(high, low_tab)


def left(x, high_tab, low_tab):
    high, low = split(x)
    return dot(high_tab, high) + dot(high_tab, low) + dot(low_tab, high)


def halves(x, axis):
    half = x.shape[axis] // 2
    return lax.slice_in_dim(x, 0, half, axis=axis), lax.slice_in_dim(x, half, 2 * half, axis=axis)


def join(parts, axis):
    return jnp.concatenate(parts, axis=axis)


def forward(mul, axis, a, b, tabs):
    (a0, a1), (b0, b1) = halves(a, axis), halves(b, axis)
    even = mul(join([a0 + a1, b0 + b1], axis), tabs[0], tabs[1])
    odd = mul(join([a0 - a1, b0 - b1], axis), tabs[2], tabs[3])
    (a0, b0), (a1, b1) = halves(even, axis), halves(odd, axis)
    return join([a0, a1], axis), join([b0, b1], axis)


def inverse(mul, axis, a, b, tabs):
    (a0, a1), (b0, b1) = halves(a, axis), halves(b, axis)
    even = mul(join([a0, b0], axis), tabs[0], tabs[1])
    odd = mul(join([a1, b1], axis), tabs[2], tabs[3])
    (a0, b0), (a1, b1) = halves(even, axis), halves(odd, axis)
    return join([a0 + a1, a0 - a1], axis), join([b0 + b1, b0 - b1], axis)


def class_of(group, step, other, parts):
    index = (group + step) & (parts - 1)
    return index ^ 1 if other else index


def patterns_kernel(size, rows, parts, slots, notes_ref, own_ref, probe_hbm, amp_hbm, tab_hbm, near_ref, far_ref, other_near_ref, other_far_ref, re_ref, im_ref,
                    own_buf, rim_buf, probe_ref, amp_ref, tab_ref, stage, own_sems, fixed_sems, piece_sems, store_sems):
    count, group = notes_ref[0, 2 * slots], notes_ref[2, 0]
    span = size + SUB
    depth = size // parts

    def start_of(p):
        return pl.multiple_of(notes_ref[0, p] & -SUB, SUB)

    def first_of(p):
        return pl.multiple_of(jnp.minimum(start_of(p), rows - span), SUB)

    def loads(p):
        slot = 2 * lax.rem(p >> 1, 2)
        return [
            pltpu.make_async_copy(
                own_ref.at[:, pl.ds(first_of(jnp.minimum(p + n, count - 1)), span)], own_buf.at[slot + n], own_sems.at[slot + n])
            for n in range(2)
        ]

    def stores(n):
        where = pl.ds(pl.multiple_of(n * 2 * depth, 2 * depth), 2 * depth)
        return [
            pltpu.make_async_copy(stage.at[ch, :, where], ref.at[:, where], store_sems.at[ch, n])
            for ch, ref in enumerate((re_ref, im_ref))
        ]

    fixed = [
        pltpu.make_async_copy(a, b, fixed_sems.at[n])
        for n, (a, b) in enumerate(((probe_hbm, probe_ref), (tab_hbm, tab_ref), (amp_hbm, amp_ref)))
    ]
    rims = []
    for other, refs in enumerate(((near_ref, far_ref), (other_near_ref, other_far_ref))):
        for n, step in enumerate(STEPS):
            index = class_of(group, step, other, parts)
            rims.append(pltpu.make_async_copy(refs[n // 2].at[n % 2], rim_buf.at[:, :, index], piece_sems.at[len(rims)]))
    for copy in loads(0) + rims + fixed:
        copy.start()

    lane = lax.broadcasted_iota(jnp.int32, (SUB, size), 1)
    head_row = lax.broadcasted_iota(jnp.int32, (SUB, size), 0)
    column = lax.broadcasted_iota(jnp.int32, (size, size), 1)
    note = jnp.zeros((SUB, size), jnp.int32)
    for side in range(2):
        for n in range(2 * slots + 1):
            note = jnp.where(jnp.logical_and(head_row == side, lane == n), notes_ref[side, n], note)
    note = note.astype(jnp.float32)
    for part in range(parts):
        stage[0, part, slots * depth :] = note
    notes = pl.ds(slots * depth, SUB)
    last = pltpu.make_async_copy(stage.at[0, :, notes], re_ref.at[:, notes], store_sems.at[0, slots])
    last.start()
    for copy in fixed + rims:
        copy.wait()
    rim = rim_buf.reshape(2, rows, size)

    def moved_down(ref, shift):
        blocks = [pltpu.roll(ref[SUB * n : SUB * (n + 1)], shift, 0) for n in range(size // SUB)]
        return jnp.concatenate([jnp.where(head_row >= shift, here, above) for here, above in zip(blocks, blocks[-1:] + blocks)], axis=0)

    def prepare(p, slot):
        row, col = notes_ref[0, p], notes_ref[0, slots + p]
        base = start_of(p)
        shift = row - base
        pr, pi = [pltpu.roll(moved_down(probe_ref.at[ch], shift), col, 1) for ch in range(2)]
        mine = column >= col
        lead = pl.multiple_of(base - first_of(p), SUB)
        tail = pl.multiple_of(jnp.minimum(lead + size, size), SUB)
        tail_rim = pl.multiple_of(jnp.minimum(base + size, rows - SUB), SUB)

        def window(ch):
            full = jnp.where(mine, own_buf[slot, ch, pl.ds(lead, size)], rim[ch, pl.ds(base, size)])
            wrap = jnp.where(mine[:SUB], own_buf[slot, ch, pl.ds(tail, SUB)], rim[ch, pl.ds(tail_rim, SUB)])
            head = jnp.where(head_row >= shift, full[:SUB], wrap)
            return jnp.concatenate([head, full[SUB:]], axis=0)

        o_re, o_im = window(0), window(1)
        return base, pr, pi, pr * o_re - pi * o_im, pr * o_im + pi * o_re

    def constrain(p, a, b):
        factor = amp_ref[p].astype(jnp.float32) * lax.rsqrt(jnp.maximum(a * a + b * b, FLOOR * FLOOR)) - 1.0
        return a * factor, b * factor

    def put(p, base, pr, pi, a, b):
        for ch, g in enumerate((pr * a + pi * b, pr * b - pi * a)):
            for t in range(parts):
                index = ((base >> 3) + t) & (parts - 1)
                for m in range(depth // SUB):
                    at = pl.multiple_of(p * depth + SUB * m, SUB)
                    block = SUB * (parts * m + t)
                    stage[ch, index, pl.ds(at, SUB)] = g[block : block + SUB]

    def pair(n, _):
        first = 2 * n
        second = jnp.minimum(first + 1, count - 1)

        @pl.when(first + 2 < count)
        def _():
            for copy in loads(first + 2):
                copy.start()

        for copy in loads(first):
            copy.wait()
        slot = 2 * lax.rem(n, 2)
        work = [(first, slot), (second, slot + 1)]
        states = [prepare(p, at) for p, at in work]
        waves = [state[3:] for state in states]
        tabs = [[tab_ref[4 * stage + n] for n in range(4)] for stage in range(4)]
        waves = [forward(right, 1, *wave, tabs[0]) for wave in waves]
        waves = [forward(left, 0, *wave, tabs[1]) for wave in waves]
        waves = [constrain(p, *wave) for (p, _), wave in zip(work, waves)]
        waves = [inverse(left, 0, *wave, tabs[2]) for wave in waves]
        waves = [inverse(right, 1, *wave, tabs[3]) for wave in waves]
        for (p, _), state, wave in zip(work, states, waves):
            put(p, *state[:3], *wave)
        for copy in stores(n):
            copy.start()
        return 0

    pairs = (count + 1) >> 1
    lax.fori_loop(0, pairs, pair, 0)

    def stored(n, _):
        for copy in stores(n):
            copy.wait()
        return 0

    last.wait()
    lax.fori_loop(0, pairs, stored, 0)


def ordered_kernel(order_ref, turned_ref, amp_ref, out_ref):
    order, turned = order_ref[...], turned_ref[...]
    for p in range(amp_ref.shape[0]):
        rows = dot(order, amp_ref[p]).astype(jnp.bfloat16)
        out_ref[p] = dot(rows, turned).astype(jnp.bfloat16)


def ordered(amplitudes):
    size = amplitudes.shape[1]
    order = np.zeros((size, size), np.float32)
    order[np.arange(size), np.concatenate([np.arange(0, size, 2), np.arange(1, size, 2)])] = 1.0
    vmem = pl.BlockSpec(memory_space=pltpu.VMEM)
    return pl.pallas_call(
        ordered_kernel,
        out_shape=jax.ShapeDtypeStruct(amplitudes.shape, amplitudes.dtype),
        in_specs=[vmem] * 3,
        out_specs=vmem,
        compiler_params=pltpu.CompilerParams(vmem_limit_bytes=16 * MIB),
        cost_estimate=pl.CostEstimate(flops=2**28, bytes_accessed=2 * MIB, transcendentals=0),
        name="ordered",
    )(jnp.asarray(order, jnp.bfloat16), jnp.asarray(order.T, jnp.bfloat16), amplitudes)


def patterns(notes, own, shares, probe, amplitudes):
    rows, size = own.shape[1:]
    slots, parts = amplitudes.shape[0], 2 * len(STEPS)
    depth = size // parts
    length = slots * depth
    smem = pl.BlockSpec(memory_space=pltpu.SMEM)
    anywhere = pl.BlockSpec(memory_space=pl.ANY)
    hbm = pl.BlockSpec(memory_space=pltpu.HBM)
    tab = jnp.asarray(tables(size))
    return pl.pallas_call(
        functools.partial(patterns_kernel, size, rows, parts, slots),
        out_shape=[jax.ShapeDtypeStruct((parts, length + extra, size), jnp.float32) for extra in (SUB, 0)],
        in_specs=[smem] + [hbm] * 4 + [anywhere] * 4,
        out_specs=[anywhere] * 2,
        scratch_shapes=[
            pltpu.VMEM((4, 2, size + SUB, size), jnp.float32),
            pltpu.VMEM((2, rows // (SUB * parts), parts, SUB, size), jnp.float32),
            pltpu.VMEM(probe.shape, jnp.float32),
            pltpu.VMEM(amplitudes.shape, amplitudes.dtype),
            pltpu.VMEM(tab.shape, tab.dtype),
            pltpu.VMEM((2, parts, length + SUB, size), jnp.float32),
            pltpu.SemaphoreType.DMA((4,)),
            pltpu.SemaphoreType.DMA((3,)),
            pltpu.SemaphoreType.DMA((parts,)),
            pltpu.SemaphoreType.DMA((2, slots + 1)),
        ],
        compiler_params=pltpu.CompilerParams(vmem_limit_bytes=40 * MIB),
        cost_estimate=pl.CostEstimate(flops=24 * 2 * size**3 * slots, bytes_accessed=12 * MIB, transcendentals=0),
        name="patterns",
    )(notes, own, probe, amplitudes, tab, *shares)


def place(row, group, parts):
    block = row >> 3
    first = (group - block) & (parts - 1)
    local = (block + first - group) >> (parts.bit_length() - 1)
    return first, pl.multiple_of(local * SUB, SUB), jnp.where(first == 0, row & (SUB - 1), 0)


def each_live(notes_ref, slots, step):
    def device(d, _):
        def pattern(p, _):
            step(d, p, notes_ref[d, p], notes_ref[d, slots + p])
            return 0

        return lax.fori_loop(0, notes_ref[d, 2 * slots], pattern, 0)

    lax.fori_loop(0, notes_ref.shape[0], device, 0)


def gather_kernel(size, parts, slots, group_ref, notes_ref, got_ref, here_ref, next_ref, total):
    depth = size // parts
    group = group_ref[0]
    total[...] = jnp.zeros_like(total)
    column = lax.broadcasted_iota(jnp.int32, (depth, size), 1)
    head_row = lax.broadcasted_iota(jnp.int32, (SUB, size), 0)

    def step(d, p, row, col):
        _, at, shift = place(row, group, parts)
        mine = column >= col
        block = got_ref[d, pl.ds(pl.multiple_of(p * depth, depth), depth)]
        for side in range(2):
            part = jnp.where(mine if side == 0 else jnp.logical_not(mine), block, 0.0)
            head = part[:SUB]
            total[side, pl.ds(at, SUB)] += jnp.where(head_row >= shift, head, 0.0)
            total[side, pl.ds(at + SUB, depth - SUB)] += part[SUB:]
            total[side, pl.ds(at + depth, SUB)] += jnp.where(head_row < shift, head, 0.0)

    each_live(notes_ref, slots, step)
    kept = here_ref.shape[0]
    here_ref[...] = total[0, :kept]
    next_ref[...] = total[1, :kept]


def gathered(group, notes, got, slots, kept):
    parts, _, size = got.shape
    smem = pl.BlockSpec(memory_space=pltpu.SMEM)
    vmem = pl.BlockSpec(memory_space=pltpu.VMEM)
    shape = jax.ShapeDtypeStruct((kept, size), jnp.float32)
    return pl.pallas_call(
        functools.partial(gather_kernel, size, parts, slots),
        out_shape=(shape, shape),
        in_specs=[smem, smem, vmem],
        out_specs=(vmem, vmem),
        scratch_shapes=[pltpu.VMEM((2, kept + SUB, size), jnp.float32)],
        compiler_params=pltpu.CompilerParams(vmem_limit_bytes=8 * MIB),
        cost_estimate=pl.CostEstimate(flops=2**21, bytes_accessed=3 * MIB, transcendentals=0),
        name="gathered",
    )(group, notes, got)


def illumination_kernel(size, parts, slots, group_ref, here_ref, before_ref, probe_ref, out_ref, intensity, total):
    depth = size // parts
    group = group_ref[0]
    square = probe_ref[0] * probe_ref[0] + probe_ref[1] * probe_ref[1]
    intensity[:SUB] = square[size - SUB :]
    intensity[SUB:] = square
    total[...] = jnp.zeros_like(total)
    column = lax.broadcasted_iota(jnp.int32, (depth, size), 1)
    head_row = lax.broadcasted_iota(jnp.int32, (SUB, size), 0)

    for side, ref in enumerate((here_ref, before_ref)):

        def step(d, p, row, col):
            first, at, shift = place(row, group, parts)
            down = row & (SUB - 1)
            blocks = []
            for m in range(depth // SUB):
                start = pl.multiple_of((parts * m + first) * SUB, SUB)
                above, below = [pltpu.roll(intensity[pl.ds(start + n * SUB, SUB)], down, 0) for n in range(2)]
                blocks.append(jnp.where(head_row >= down, below, above))
            placed = pltpu.roll(jnp.concatenate(blocks, axis=0), col, 1)
            part = jnp.where(column >= col if side == 0 else column < col, placed, 0.0)
            head = part[:SUB]
            total[pl.ds(at, SUB)] += jnp.where(head_row >= shift, head, 0.0)
            total[pl.ds(at + SUB, depth - SUB)] += part[SUB:]
            total[pl.ds(at + depth, SUB)] += jnp.where(head_row < shift, head, 0.0)

        each_live(ref, slots, step)
    out_ref[...] = total[: out_ref.shape[0]] + REG


def illumination(group, here, before, probe, slots, kept):
    size = probe.shape[1]
    parts = here.shape[0]
    smem = pl.BlockSpec(memory_space=pltpu.SMEM)
    vmem = pl.BlockSpec(memory_space=pltpu.VMEM)
    return pl.pallas_call(
        functools.partial(illumination_kernel, size, parts, slots),
        out_shape=jax.ShapeDtypeStruct((kept, size), jnp.float32),
        in_specs=[smem, smem, smem, vmem],
        out_specs=vmem,
        scratch_shapes=[
            pltpu.VMEM((size + SUB, size), jnp.float32),
            pltpu.VMEM((kept + SUB, size), jnp.float32),
        ],
        compiler_params=pltpu.CompilerParams(vmem_limit_bytes=4 * MIB),
        cost_estimate=pl.CostEstimate(flops=2**22, bytes_accessed=8 * MIB, transcendentals=0),
        name="illumination",
    )(group, here, before, probe)


def assemble_kernel(kinds, parts, staged, group_ref, *refs):
    sources, loads = list(refs[: len(kinds)]), {}
    if staged:
        out_ref, held, load_sems, sems = refs[-4:]
        for n, k in enumerate(staged):
            loads[k] = pltpu.make_async_copy(sources[k], held.at[n], load_sems.at[n])
            loads[k].start()
            sources[k] = held.at[n]
    else:
        out_ref, sems = refs[-2:]
    copies = []
    for k, (ch, other) in enumerate(kinds):
        core = (group_ref[0] & 1) ^ other
        if k in loads:
            loads[k].wait()
        for n in range(parts // 2):
            copies.append(pltpu.make_async_copy(sources[k].at[n], out_ref.at[ch, :, 2 * n + core], sems.at[len(copies)]))
            copies[-1].start()
    for copy in copies:
        copy.wait()


def assembled(group, kinds, shares, shape, begun=(), staged=()):
    parts = shape[2]
    anywhere = pl.BlockSpec(memory_space=pl.ANY)
    hbm = pl.BlockSpec(memory_space=pltpu.HBM)
    count = len(shares)
    held = [pltpu.VMEM((len(staged), *shares[0].shape), jnp.float32), pltpu.SemaphoreType.DMA((len(staged),))] if staged else []
    return pl.pallas_call(
        functools.partial(assemble_kernel, kinds, parts, staged),
        out_shape=jax.ShapeDtypeStruct(shape, jnp.float32),
        in_specs=[pl.BlockSpec(memory_space=pltpu.SMEM)] + [anywhere] * count + [hbm] * len(begun),
        out_specs=hbm,
        scratch_shapes=held + [pltpu.SemaphoreType.DMA((count * parts // 2,))],
        input_output_aliases={1 + count: 0} if begun else {},
        compiler_params=pltpu.CompilerParams(vmem_limit_bytes=5 * MIB if staged else MIB),
        cost_estimate=pl.CostEstimate(flops=0, bytes_accessed=2 * count * MIB, transcendentals=0),
        name="assembled",
    )(group, *shares, *begun)


def passed_along(x, axis, by):
    devices = lax.axis_size(axis)
    pairs = [(i, i + by) for i in range(devices) if 0 <= i + by < devices]
    return lax.ppermute(x, axis, pairs)


def to_chip(x, by):
    devices = lax.axis_size("group")
    return lax.ppermute(x, "group", [(i, (i + 2 * by) % devices) for i in range(devices)])


def to_core(x):
    return lax.ppermute(x, "group", [(i, i ^ 1) for i in range(lax.axis_size("group"))])


def body(object_field, probe, amplitudes, row_offset, col_offset, counts):
    parts = lax.axis_size("group")
    index = lax.axis_index("group")
    group = index[None]
    rows, size = object_field.shape[1:]
    slots = amplitudes.shape[0]
    kept = rows // parts
    blocks = object_field.reshape(2, kept // SUB, parts, SUB, size)

    def cut(source, which):
        return lax.dynamic_index_in_dim(source, which, 2, keepdims=False)

    own_notes = jnp.concatenate([row_offset, col_offset, counts])
    far = passed_along(jnp.stack([cut(blocks, (index + 4) % parts), cut(blocks, (index + 2) % parts)]), "tile", -1)
    near, notes_before = lax.optimization_barrier((passed_along(cut(blocks, index), "tile", -1), passed_along(own_notes, "tile", 1)))
    near = jnp.stack([near, to_chip(near, 1)])
    notes = jnp.stack([own_notes, notes_before, jnp.full_like(own_notes, index)])
    sent = patterns(notes, object_field, (near, far, to_core(near), to_core(far)), probe, ordered(amplitudes))
    blocks, first = lax.optimization_barrier((blocks, sent[0]))
    sent = (first, sent[1])
    mine = cut(blocks, index)
    gots = [lax.all_to_all(channel, "group", 0, 0) for channel in sent]
    notes = gots[0][:, slots * (size // parts) :, : 2 * slots + 1].astype(jnp.int32)
    notes_here, notes_before = notes[:, 0], notes[:, 1]
    weight = illumination(group, notes_here, notes_before, probe, slots, kept)
    chips = parts // 2
    same_core = [list(range(core, parts, 2)) for core in range(2)]
    spreads = []
    for ch, got in enumerate(gots):
        here, spill = gathered(group, notes_here, got, slots, kept)
        spill = passed_along(spill, "tile", 1)
        if spreads:
            spill, _ = lax.optimization_barrier((spill, spreads[0]))
        result = mine[ch] + ((here + spill) / weight).reshape(mine.shape[1:])
        spreads.append(jnp.broadcast_to(result, (chips, *result.shape)))
    shares = [lax.all_to_all(spreads[0], "group", 0, 0, axis_index_groups=same_core)]
    shares[0], spreads[1] = lax.optimization_barrier((shares[0], spreads[1]))
    shares.append(lax.all_to_all(spreads[1], "group", 0, 0, axis_index_groups=same_core))
    field = assembled(group, ((0, 0),), shares[:1], blocks.shape, staged=(0,))
    shares[1], field = lax.optimization_barrier((shares[1], field))
    others = [to_core(share) for share in shares]
    field = assembled(group, ((1, 0), (0, 1)), (shares[1], others[0]), blocks.shape, (field,), staged=(1,))
    field = assembled(group, ((1, 1),), (others[1],), blocks.shape, (field,))
    return field.reshape(object_field.shape)


def solution(mesh):
    in_specs = (
        P(None, None, "tile"),
        P(),
        P(("tile", "group"), None, None),
        P(("tile", "group")),
        P(("tile", "group")),
        P(("tile", "group")),
    )
    out_specs = P(None, None, "tile")
    return jax.shard_map(body, mesh=mesh, in_specs=in_specs, out_specs=out_specs, check_vma=False)
```
